256 devices in a mesh: dp: 128 (over z, y, x_lo, core), tensor: 2 (over x_hi).
Axes of the slice: x: 4 (x_hi: 2, x_lo: 2; x = x_hi * 2 + x_lo), y: 4, z: 8, core: 2. Of those that a mesh axis runs over, the one named last changes fastest.
Arguments:
- source_frames: bfloat16 [32768, 1536], P(('dp', 'tensor')), may hold values from -24 to 24
- routes: int32 [32768, 1], P(('dp', 'tensor')), may hold values from 0 to 127; in each aligned block of 128 rows (0 to 127, 128 to 255, ...) at most 2 rows name the same one
- live_frames: int32 [256], P(('dp', 'tensor')), may hold values from 32 to 128
- norm_gain: float32 [1536], replicated, may hold values from 0.1 to 1.9
- weight_in: bfloat16 [1536, 3072], P(None, 'tensor'), may hold values from -0.15625 to 0.15625
- weight_out: bfloat16 [3072, 1536], P('tensor'), may hold values from -0.109375 to 0.109375
- cotangent: bfloat16 [65536, 1536], P(('dp', 'tensor')), may hold values from -24 to 24
Outputs:
- mixed: bfloat16 [65536, 1536], P(('dp', 'tensor'))
- grad_source: bfloat16 [32768, 1536], P(('dp', 'tensor'))
- grad_out: float32 [3072, 1536], P('tensor', 'dp')
The draws below stay inside these ranges and needn't reach their ends.
Inputs may be any that keep to these rules, and one draw needn't show every extreme that they name: `routes`: among the slots of one device, no destination index is named by more than 2 slots, a bound that some block reaches.
All inputs are finite; a program needn't handle non-finite values.
Results may differ from the reference program's by a relative error of at most 0.008.
Values may be sent and summed in bfloat16 or wider, within the bound.
A program may use at most 128 MiB of HBM per device.

```python
import math
import jax
import jax.numpy as jnp
import numpy as np
from jax import lax

D = 1536
H = 3072
FR_SRC = 128
DST_ROWS = 256
CAP = 2
SRC_TOTAL = 32768
DST_TOTAL = 65536
N_DP = 128
N_TENSOR = 2


def touch_ends(values, stream_key, low, top_value):
    index_at = [jax.random.randint(jax.random.fold_in(stream_key, axis), (), 0, length) for axis, length in enumerate(values.shape)]
    widest = values.shape.index(max(values.shape))
    beside = index_at[:widest] + [(index_at[widest] + 1) % values.shape[widest]] + index_at[widest + 1:]
    return values.at[tuple(index_at)].set(low).at[tuple(beside)].set(top_value)


def with_spikes(values, rng, source, target, parts, factor):
    owner, partner = [(jnp.arange(values.shape[axis_at]) // (values.shape[axis_at] // parts)).reshape([-1 if axis == axis_at else 1 for axis in range(values.ndim)]) for axis_at in (source, target)]
    chosen = jax.random.permutation(rng, parts)[partner]
    strong = (owner == chosen) | (owner == (partner + parts // 2) % parts)
    return jnp.where(strong, factor * values, values)


def level_of(own_key, shape, pieces, low, largest):
    gain = 1.0
    for axis_at, blocks in pieces:
        steps = jax.random.uniform(jax.random.fold_in(jax.random.fold_in(own_key, 6), axis_at), (blocks,), jnp.float32, low / len(pieces), largest / len(pieces))
        gain = gain * jnp.repeat(jnp.exp(steps), shape[axis_at] // blocks).reshape((-1,) + (1,) * (len(shape) - 1 - axis_at))
    return gain


def routed_block(rng, own, number, rows, count, top, reach, slope):
    sequence = jax.random.permutation(rng, count)
    crowded, common = load_shares(count, rows * top, reach, slope, True), load_shares(count, rows * top, reach, slope, False)
    places = jnp.arange(count)

    def named(sizes, turn):
        used = int((sizes > 0).sum())
        fixed = max(1, used // 4)
        passed = fixed + (places - fixed + turn * (used - fixed)) % max(1, count - fixed)
        return jnp.zeros((count,), jnp.int32).at[sequence[jnp.where(places < fixed, places, passed)]].set(jnp.asarray(sizes, jnp.int32))

    sizes = jnp.where(number % 4 == 0, named(crowded, number // 4), named(common, number - number // 4 - 1))
    mixed = jax.random.permutation(jax.random.fold_in(own, 3), count)
    giver, taker = mixed[0:count // 2 * 2:2], mixed[1:count // 2 * 2:2]
    slack = jnp.minimum(sizes[giver] - 1, reach - sizes[taker]) // 2
    slack = jnp.where((giver == sequence[0]) | (taker == sequence[0]) | (sizes[taker] == 0), 0, jnp.maximum(slack, 0))
    passed = jax.random.randint(jax.random.fold_in(own, 4), (count // 2,), 0, 1 << 20) % (slack + 1)
    sizes = sizes.at[giver].add(-passed).at[taker].add(passed)
    items = jnp.searchsorted(jnp.cumsum(sizes), jnp.arange(rows * top), side="right").astype(jnp.int32)
    grid = items.reshape(top, rows).T
    grid = grid[jax.random.permutation(jax.random.fold_in(own, 1), rows)]
    turn = jax.random.randint(jax.random.fold_in(own, 2), (rows, 1), 0, top)
    return jnp.take_along_axis(grid, (jnp.arange(top)[None, :] + turn) % top, axis=1)


def load_shares(amount, total, most, lean, full):
    weights = [(1 << 20) // math.isqrt(standing ** lean) + 1 for standing in range(1, amount + 1)]
    largest = most if full else min(most, max(-(-total // amount), total * weights[0] // sum(weights)))
    least = 1 if total - largest >= amount - 1 else 0
    counts, rest = [largest] + [least] * (amount - 1), total - largest - least * (amount - 1)
    while rest > 0:
        candidates = [i for i in range(1, amount) if counts[i] < largest] or [i for i in range(1, amount) if counts[i] < most]
        mass, budget = sum([weights[i] for i in candidates]), rest
        for i in candidates:
            addition = min(most - counts[i], max(1, budget * weights[i] // mass), rest)
            counts[i] = counts[i] + addition
            rest = rest - addition
    return np.array(counts)


def normal_values(key, dims, deviation, most, shards=(), held_as=jnp.bfloat16):
    result = jax.random.normal(key, dims, jnp.float32) * deviation
    if len(shards) > 0:
        result = level_of(key, dims, shards, -0.22, 0.18) * result
    return jnp.clip(result, min=-most, max=most).astype(held_as)


def noise_with(key, extent, spread, bound, pieces, heavy, kind=jnp.bfloat16):
    result = spread * jax.random.normal(key, extent, jnp.float32)
    if pieces:
        result = result * level_of(key, extent, pieces, -0.22, 0.18)
    return jnp.clip(with_spikes(result, jax.random.fold_in(key, 3), *heavy), -bound, bound).astype(kind)


def setup_inputs(seed: int = 0) -> dict:
    key_list = jax.random.split(jax.random.key(seed), 8)
    source_frames = noise_with(key_list[0], (SRC_TOTAL, D), 1.0, 24.0, ((0, 256),), (0, 1, 256, 6.0))
    routes_keys = jax.random.split(jax.random.fold_in(key_list[1], 1), SRC_TOTAL // FR_SRC)
    routes_turns = jax.random.permutation(jax.random.fold_in(key_list[1], 3), SRC_TOTAL // FR_SRC)
    routes = jax.vmap(lambda own, number: routed_block(jax.random.fold_in(key_list[1], 2), own, number, FR_SRC, N_DP, 1, CAP, 1))(routes_keys, routes_turns).reshape((SRC_TOTAL, 1))
    live_frames = touch_ends(jax.random.randint(key_list[2], (N_DP * N_TENSOR,), FR_SRC // 4, FR_SRC + 1), jax.random.fold_in(key_list[2], 1), FR_SRC // 4, FR_SRC).astype(jnp.int32)
    norm_gain = jnp.clip(1.0 + 0.18 * jax.random.normal(key_list[3], (D,), jnp.float32), 0.1, 1.9)
    weight_in = normal_values(key_list[4], (D, H), D ** -0.5, 0.15625, ((1, 2),))
    weight_out = normal_values(key_list[5], (H, D), H ** -0.5, 0.109375, ((0, 2),))
    cotangent = noise_with(key_list[6], (DST_TOTAL, D), 1.0, 24.0, ((0, 256),), (0, 1, 256, 6.0))
    return {"source_frames": source_frames, "routes": routes, "live_frames": live_frames, "norm_gain": norm_gain, "weight_in": weight_in, "weight_out": weight_out, "cotangent": cotangent}


epsilon = 1e-05

def rounded(value):
    return lax.optimization_barrier(value.astype(jnp.bfloat16)).astype(jnp.float32)

def group_sum(left, right_mat):
    group = H // N_TENSOR
    total = jnp.zeros((left.shape[0], right_mat.shape[1]), jnp.float32)
    for index in range(N_TENSOR):
        piece = jnp.dot(left[:, index * group:(index + 1) * group], right_mat[index * group:(index + 1) * group, :], preferred_element_type=jnp.float32)
        total = total + rounded(piece)
    return total

def block_pass(frames, grads, norm_gain, weight_in, weight_out):
    frames_f = frames.astype(jnp.float32)
    row_mean = lax.optimization_barrier(jnp.mean(frames_f, axis=1, keepdims=True))
    centred = frames_f - row_mean
    row_var = lax.optimization_barrier(jnp.mean(centred * centred, axis=1, keepdims=True))
    inv_std = lax.rsqrt(row_var + epsilon)
    normed = centred * inv_std
    scaled = (normed * norm_gain).astype(jnp.bfloat16)
    hidden = jnp.dot(scaled, weight_in, preferred_element_type=jnp.float32)
    sigmoid_gate = jax.nn.sigmoid(hidden)
    activated = (hidden * sigmoid_gate).astype(jnp.bfloat16)
    mixed_sum = group_sum(activated, weight_out)
    output_rows = (frames_f + 0.5 * mixed_sum).astype(jnp.bfloat16)
    grad_act = 0.5 * jnp.dot(grads, weight_out.T, preferred_element_type=jnp.float32)
    grad_hidden = (grad_act * sigmoid_gate * (1.0 + hidden * (1.0 - sigmoid_gate))).astype(jnp.bfloat16)
    grad_out = 0.5 * jnp.dot(activated.T, grads, preferred_element_type=jnp.float32)
    grad_scaled = group_sum(grad_hidden, weight_in.T)
    grad_normed = grad_scaled * norm_gain
    first_mean = lax.optimization_barrier(jnp.mean(grad_normed, axis=1, keepdims=True))
    second_mean = lax.optimization_barrier(jnp.mean(grad_normed * normed, axis=1, keepdims=True))
    grad_rows = (grads.astype(jnp.float32) + inv_std * (grad_normed - first_mean - normed * second_mean)).astype(jnp.bfloat16)
    return (output_rows, grad_rows, grad_out)

def reference(source_frames, routes, live_frames, norm_gain, weight_in, weight_out, cotangent):
    device_count = N_DP * N_TENSOR
    target = routes[:, 0].reshape(device_count, FR_SRC)
    one_hot = (target[:, :, None] == jnp.arange(N_DP, dtype=jnp.int32)[None, None, :]).astype(jnp.int32)
    before = jnp.cumsum(one_hot, axis=1) - one_hot
    slot_rank = lax.optimization_barrier(jnp.sum(before * one_hot, axis=2)).astype(jnp.int32)
    device = jnp.arange(device_count, dtype=jnp.int32)[:, None]
    dest_row = ((target * N_TENSOR + device % N_TENSOR) * DST_ROWS + device // N_TENSOR * CAP + slot_rank).reshape(-1).astype(jnp.int32)
    alive_mask = (jnp.arange(FR_SRC, dtype=jnp.int32)[None, :] < live_frames[:, None]).reshape(-1, 1)
    alive_frames = jnp.where(alive_mask, source_frames, jnp.zeros_like(source_frames))
    frames = jnp.zeros((DST_TOTAL, D), jnp.bfloat16).at[dest_row].set(alive_frames)
    present = jnp.zeros((DST_TOTAL, 1), jnp.int32).at[dest_row].set(alive_mask.astype(jnp.int32))
    grads = jnp.where(present > 0, cotangent, jnp.zeros_like(cotangent))
    group_rows = N_TENSOR * DST_ROWS
    frame_blocks = frames.reshape(N_DP, group_rows, D)
    grad_blocks = grads.reshape(N_DP, group_rows, D)

    def step_block(carry, pair):
        output_rows, grad_rows, grad_out = block_pass(pair[0], pair[1], norm_gain, weight_in, weight_out)
        return (carry + grad_out, (output_rows, grad_rows))
    total, stacked = lax.scan(step_block, jnp.zeros((H, D), jnp.float32), (frame_blocks, grad_blocks))
    mixed = stacked[0].reshape(-1, D)
    grad_all = stacked[1].reshape(-1, D)
    picked = grad_all[dest_row]
    grad_source = jnp.where(alive_mask, picked, jnp.zeros_like(picked))
    return (mixed, grad_source, total)
```

```python
import functools

import jax
import jax.numpy as jnp
from jax import lax
from jax.experimental import pallas as pl
from jax.experimental.pallas import tpu as pltpu
from jax.sharding import PartitionSpec as P

epsilon = 1e-05
ABSENT = 64.0
MESH = pl.DeviceIdType.MESH
GROUP = 16


def on_dp(index):
    return {"dp": index}


def remote(src, dst, send_sem, recv_sem, index):
    return pltpu.make_async_remote_copy(
        src_ref=src,
        dst_ref=dst,
        send_sem=send_sem,
        recv_sem=recv_sem,
        device_id=on_dp(index),
        device_id_type=MESH,
    )


class Exchange:
    def __init__(self, n, place, device_of, src, dst, send_sem, recv_sem):
        self.n, self.place, self.device_of = n, place, device_of
        self.src, self.dst, self.send_sem, self.recv_sem = src, dst, send_sem, recv_sem

    def after(self, offset):
        return lax.rem(self.place + offset, self.n)

    def before(self, offset):
        return lax.rem(self.place + self.n - offset, self.n)

    def _out(self, offset):
        p = self.after(offset)
        return remote(
            self.src.at[p],
            self.dst.at[self.place],
            self.send_sem.at[p],
            self.recv_sem.at[self.place],
            self.device_of(p),
        )

    def start(self, offset):
        self._out(offset).start()

    def wait_send(self, offset):
        self._out(offset).wait_send()

    def wait_recv(self, offset):
        p = self.before(offset)
        remote(
            self.src.at[p], self.dst.at[p], self.send_sem.at[p], self.recv_sem.at[p], self.device_of(p)
        ).wait_recv()

    def each(self, method):
        @pl.loop(1, self.n)
        def _(offset):
            method(offset)

    def run(self):
        self.each(self.start)
        self.dst[self.place] = self.src[self.place]
        self.each(self.wait_recv)
        self.each(self.wait_send)


def greet(groups):
    barrier = pltpu.get_barrier_semaphore()
    total = 0
    for n, place, device_of in groups:
        @pl.loop(1, n)
        def _(offset):
            pl.semaphore_signal(
                barrier,
                inc=1,
                device_id=on_dp(device_of(lax.rem(place + offset, n))),
                device_id_type=MESH,
            )

        total += n - 1
    pl.semaphore_wait(barrier, total)


def swap_matrix(outer, inner, pair):
    n = outer * inner * pair
    row = lax.broadcasted_iota(jnp.int32, (n, n), 0)
    col = lax.broadcasted_iota(jnp.int32, (n, n), 1)
    i, o, r = row // (outer * pair), (row // pair) % outer, row % pair
    return (col == (o * inner + i) * pair + r).astype(jnp.bfloat16)


def swap_rows(outer, inner, pair, rows):
    return jnp.dot(
        swap_matrix(outer, inner, pair), rows, preferred_element_type=jnp.float32
    ).astype(jnp.bfloat16)


def slot_matrix(routes_ref, live_ref, slots, capacity):
    count = routes_ref.shape[1]
    target = routes_ref[...]
    row = lax.broadcasted_iota(jnp.int32, (count, count), 0)
    col = lax.broadcasted_iota(jnp.int32, (count, count), 1)
    wide = jnp.broadcast_to(target, (count, count))
    tall = jnp.sum(jnp.where(row == col, wide, 0), axis=1, keepdims=True)
    rank = jnp.sum(((tall == wide) & (row < col)).astype(jnp.int32), axis=0, keepdims=True)
    slot = target * capacity + rank
    alive = lax.broadcasted_iota(jnp.int32, (1, count), 1) < live_ref[...]
    slot = jnp.where(alive, slot, -1)
    return (lax.broadcasted_iota(jnp.int32, (slots, count), 0) == slot).astype(jnp.float32)


def dispatch_kernel(nz, capacity, frames_ref, routes_ref, live_ref, out_ref, sendz, recvz, sendj, recvj, sz, rz, sj, rj):
    me = lax.axis_index("dp")
    z, j = me // GROUP, lax.rem(me, GROUP)
    z_device = lambda p: p * GROUP + j
    j_device = lambda p: z * GROUP + p
    greet([(nz, z, z_device), (GROUP, j, j_device)])
    slots = nz * GROUP * capacity
    width = frames_ref.shape[1]
    hot = slot_matrix(routes_ref, live_ref, slots, capacity)
    empty = jnp.sum(hot, axis=1, keepdims=True) < 0.5
    rows = jnp.dot(hot.astype(jnp.bfloat16), frames_ref[...], preferred_element_type=jnp.float32)
    first = lax.broadcasted_iota(jnp.int32, (slots, width), 1) == 0
    rows = jnp.where(empty & first, ABSENT, rows).astype(jnp.bfloat16)
    sendz[...] = rows.reshape(sendz.shape)
    Exchange(nz, z, z_device, sendz, recvz, sz, rz).run()
    rows = swap_rows(nz, GROUP, capacity, recvz[...].reshape(slots, width))
    sendj[...] = rows.reshape(sendj.shape)
    Exchange(GROUP, j, j_device, sendj, recvj, sj, rj).run()
    out_ref[...] = swap_rows(GROUP, nz, capacity, recvj[...].reshape(slots, width))


def return_kernel(nz, capacity, rows_ref, routes_ref, live_ref, out_ref, sendj, recvj, sendz, recvz, sj, rj, sz, rz):
    me = lax.axis_index("dp")
    z, j = me // GROUP, lax.rem(me, GROUP)
    z_device = lambda p: p * GROUP + j
    j_device = lambda p: z * GROUP + p
    greet([(nz, z, z_device), (GROUP, j, j_device)])
    slots, width = rows_ref.shape
    sendj[...] = swap_rows(nz, GROUP, capacity, rows_ref[...]).reshape(sendj.shape)
    Exchange(GROUP, j, j_device, sendj, recvj, sj, rj).run()
    rows = swap_rows(GROUP, nz, capacity, recvj[...].reshape(slots, width))
    sendz[...] = rows.reshape(sendz.shape)
    Exchange(nz, z, z_device, sendz, recvz, sz, rz).run()
    hot = slot_matrix(routes_ref, live_ref, slots, capacity).astype(jnp.bfloat16)
    out_ref[...] = lax.dot_general(
        hot,
        recvz[...].reshape(slots, width),
        (((0,), (0,)), ((), ())),
        preferred_element_type=jnp.float32,
    ).astype(jnp.bfloat16)


def vmem_specs(n):
    return [pl.BlockSpec(memory_space=pltpu.VMEM)] * n


def move_rows(kernel, name, collective_id, out_rows, z_first, rows, routes_row, live, ndp, capacity):
    nz = ndp // GROUP
    width = rows.shape[1]
    by_z = pltpu.VMEM((nz, GROUP * capacity, width), jnp.bfloat16)
    by_j = pltpu.VMEM((GROUP, nz * capacity, width), jnp.bfloat16)
    dma = pltpu.SemaphoreType.DMA
    sems_z, sems_j = [dma((nz,))] * 2, [dma((GROUP,))] * 2
    scratch = [by_z, by_z, by_j, by_j] + sems_z + sems_j if z_first else [by_j, by_j, by_z, by_z] + sems_j + sems_z
    return pl.pallas_call(
        functools.partial(kernel, nz, capacity),
        out_shape=jax.ShapeDtypeStruct((out_rows, width), jnp.bfloat16),
        in_specs=vmem_specs(3),
        out_specs=vmem_specs(1)[0],
        scratch_shapes=scratch,
        compiler_params=pltpu.CompilerParams(
            collective_id=collective_id, has_side_effects=True, vmem_limit_bytes=24 * 1024 * 1024
        ),
        name=name,
    )(rows, routes_row, live)


def reduce_kernel(nz, grads_ref, act_ref, out_ref, mine, sib_out, sib_in, yx_out, yx_in, z_out, z_in, last_out, last_in, ss, rs, sy, ry, sz, rz, sl, rl):
    me = lax.axis_index("dp")
    nyx = GROUP // 2
    z, yx, core = me // GROUP, lax.rem(me, GROUP) // 2, lax.rem(me, 2)
    sibling = me + 1 - 2 * core
    z_device = lambda p: p * GROUP + yx * 2 + core
    yx_device = lambda p: z * GROUP + p * 2 + core
    core_device = lambda p: z * GROUP + yx * 2 + p
    greet([(nz, z, z_device), (nyx, yx, yx_device), (2, core, core_device)])
    tile, half = mine.shape[1], mine.shape[2]

    def product(p, which):
        rows = grads_ref[pl.ds(pl.multiple_of(p * tile, tile), tile), :]
        columns = pl.ds(pl.multiple_of(which * half, half), half)
        return 0.5 * jnp.dot(rows, act_ref[:, columns], preferred_element_type=jnp.float32)

    def to_sibling(p):
        return remote(sib_out.at[p], sib_in.at[p], ss.at[p], rs.at[p], sibling)

    @pl.loop(1, nyx + 1)
    def _(offset):
        p = lax.rem(yx + offset, nyx)
        sib_out[p] = product(p, 1 - core).astype(jnp.bfloat16)
        to_sibling(p).start()

    over_yx = Exchange(nyx, yx, yx_device, yx_out, yx_in, sy, ry)

    def add_cores(offset):
        p = lax.rem(yx + offset, nyx)
        to_sibling(p).wait_recv()
        return mine[p].astype(jnp.float32) + sib_in[p].astype(jnp.float32)

    @pl.loop(1, nyx + 1)
    def _(offset):
        p = lax.rem(yx + offset, nyx)
        mine[p] = product(p, core)

    @pl.loop(1, nyx)
    def _(offset):
        p = lax.rem(yx + offset, nyx)
        yx_out[p] = add_cores(offset).astype(jnp.bfloat16)
        over_yx.start(offset)

    mine[yx] = add_cores(nyx)

    @pl.loop(1, nyx)
    def _(offset):
        over_yx.wait_recv(offset)
        mine[yx] += yx_in[over_yx.before(offset)].astype(jnp.float32)

    z_out[...] = mine[yx].astype(jnp.bfloat16).reshape(z_out.shape)
    over_z = Exchange(nz, z, z_device, z_out, z_in, sz, rz)
    over_z.each(over_z.start)
    last_out[...] = z_out[z].astype(jnp.float32)

    @pl.loop(1, nz)
    def _(offset):
        over_z.wait_recv(offset)
        last_out[...] += z_in[over_z.before(offset)].astype(jnp.float32)

    last = remote(last_out, last_in, sl.at[0], rl.at[0], sibling)
    last.start()
    last.wait_recv()
    own, other = last_out[...], last_in[...]
    rows = own.shape[0] // 2
    is_low = core == 0
    own = jnp.where(is_low, own[:rows], own[rows:])
    other = jnp.where(is_low, other[:rows], other[rows:])
    out_ref[:, :half] = jnp.where(is_low, own, other)
    out_ref[:, half:] = jnp.where(is_low, other, own)
    last.wait_send()
    over_yx.each(over_yx.wait_send)
    over_z.each(over_z.wait_send)

    @pl.loop(0, nyx)
    def _(p):
        to_sibling(p).wait_send()


def reduce_grad(grads_turned, activated, ndp):
    nz, nyx = ndp // GROUP, GROUP // 2
    width, hidden_units = grads_turned.shape[0], activated.shape[1]
    tile, half, rows = width // nyx, hidden_units // 2, width // nyx // nz
    dma = pltpu.SemaphoreType.DMA
    wide = pltpu.VMEM((nyx, tile, half), jnp.bfloat16)
    thin = pltpu.VMEM((nz, rows, half), jnp.bfloat16)
    return pl.pallas_call(
        functools.partial(reduce_kernel, nz),
        out_shape=jax.ShapeDtypeStruct((rows // 2, hidden_units), jnp.float32),
        in_specs=vmem_specs(2),
        out_specs=vmem_specs(1)[0],
        scratch_shapes=[
            pltpu.VMEM((nyx, tile, half), jnp.float32),
            wide,
            wide,
            wide,
            wide,
            thin,
            thin,
            pltpu.VMEM((rows, half), jnp.float32),
            pltpu.VMEM((rows, half), jnp.float32),
            dma((nyx,)),
            dma((nyx,)),
            dma((nyx,)),
            dma((nyx,)),
            dma((nz,)),
            dma((nz,)),
            dma((1,)),
            dma((1,)),
        ],
        compiler_params=pltpu.CompilerParams(
            collective_id=3, has_side_effects=True, vmem_limit_bytes=32 * 1024 * 1024
        ),
        name="reduce_grad",
    )(grads_turned, activated)


def local(source_frames, routes, live_frames, norm_gain, weight_in, weight_out, cotangent):
    ndp, nt = lax.axis_size("dp"), lax.axis_size("tensor")
    capacity = cotangent.shape[0] // ndp
    width = cotangent.shape[1]
    nz = ndp // GROUP
    axes = ("dp", "tensor")
    partners = [(p * nt + t, (p ^ 2) * nt + (1 - t)) for p in range(ndp) for t in range(nt)]
    swap = lambda value: lax.ppermute(value, axes, partners)
    routes_row, live = routes.reshape(1, -1), live_frames.reshape(1, 1)

    cotangent_other = swap(cotangent)
    arrived = move_rows(
        dispatch_kernel, "dispatch", 1, ndp * capacity, True, source_frames, routes_row, live, ndp, capacity
    )
    arrived_other = swap(arrived)

    def normalise(slots):
        frames = slots.astype(jnp.float32)
        present = frames[:, :1] < 0.5 * ABSENT
        frames = jnp.where(present, frames, 0.0)
        centred = frames - jnp.mean(frames, axis=1, keepdims=True)
        inv_std = lax.rsqrt(jnp.mean(centred * centred, axis=1, keepdims=True) + epsilon)
        normed = centred * inv_std
        return present, frames, inv_std, normed, (normed * norm_gain).astype(jnp.bfloat16)

    def module(scaled, grads):
        hidden = jnp.dot(scaled, weight_in, preferred_element_type=jnp.float32)
        gate = jax.nn.sigmoid(hidden)
        activated = (hidden * gate).astype(jnp.bfloat16)
        grad_act = 0.5 * lax.dot_general(
            grads, weight_out, (((1,), (1,)), ((), ())), preferred_element_type=jnp.float32
        )
        grad_hidden = (grad_act * gate * (1.0 + hidden * (1.0 - gate))).astype(jnp.bfloat16)
        grad_scaled = lax.dot_general(
            grad_hidden, weight_in, (((1,), (1,)), ((), ())), preferred_element_type=jnp.float32
        ).astype(jnp.bfloat16)
        mixed_sum = jnp.dot(activated, weight_out, preferred_element_type=jnp.float32).astype(jnp.bfloat16)
        return activated, grad_scaled, mixed_sum

    present, frames, inv_std, normed, scaled = normalise(arrived)
    present_other, _, _, _, scaled_other = normalise(arrived_other)
    grads = jnp.where(present, cotangent, 0)
    grads_other = jnp.where(present_other, cotangent_other, 0)
    activated, grad_scaled, mixed_sum = module(scaled, grads)
    activated_other, grad_scaled_other, mixed_sum_other = module(scaled_other, grads_other)
    grad_scaled_back = swap(grad_scaled_other)
    mixed_back = swap(mixed_sum_other)

    both = jnp.concatenate([grads, grads_other], axis=0)
    turned = both.reshape(-1, nz, GROUP // 2, width // nz // (GROUP // 2)).transpose(2, 1, 3, 0).reshape(width, -1)
    grad_out = reduce_grad(turned, jnp.concatenate([activated, activated_other], axis=0), ndp).T

    grad_normed = (grad_scaled.astype(jnp.float32) + grad_scaled_back.astype(jnp.float32)) * norm_gain
    first_mean = jnp.mean(grad_normed, axis=1, keepdims=True)
    second_mean = jnp.mean(grad_normed * normed, axis=1, keepdims=True)
    grad_rows = (
        grads.astype(jnp.float32) + inv_std * (grad_normed - first_mean - normed * second_mean)
    ).astype(jnp.bfloat16)
    grad_source = move_rows(
        return_kernel, "give_back", 2, source_frames.shape[0], False, grad_rows, routes_row, live, ndp, capacity
    )
    mixed = (
        frames + 0.5 * (mixed_sum.astype(jnp.float32) + mixed_back.astype(jnp.float32))
    ).astype(jnp.bfloat16)
    return (mixed, grad_source, grad_out)


def solution(mesh):
    return jax.shard_map(
        local,
        mesh=mesh,
        in_specs=(
            P(("dp", "tensor"), None),
            P(("dp", "tensor"), None),
            P(("dp", "tensor")),
            P(),
            P(None, "tensor"),
            P("tensor", None),
            P(("dp", "tensor"), None),
        ),
        out_specs=(P(("dp", "tensor"), None), P(("dp", "tensor"), None), P("tensor", "dp")),
        check_vma=False,
    )
```

```python
import functools
from types import SimpleNamespace

import jax
import jax.numpy as jnp
from jax import lax
from jax.experimental import pallas as pl
from jax.experimental.pallas import tpu as pltpu
from jax.sharding import PartitionSpec as P

epsilon = 1e-05
ABSENT = 64.0
MESH = pl.DeviceIdType.MESH
GROUP = 16
RING = 4
DMA = pltpu.SemaphoreType.DMA
BF16, F32 = jnp.bfloat16, jnp.float32


def remote(src, dst, send_sem, recv_sem, device):
    return pltpu.make_async_remote_copy(
        src_ref=src, dst_ref=dst, send_sem=send_sem, recv_sem=recv_sem, device_id=device, device_id_type=MESH
    )


class Exchange:
    def __init__(self, n, place, device_of, buffers):
        self.n, self.place, self.device_of = n, place, device_of
        self.src, self.dst, self.send_sem, self.recv_sem = buffers

    def _out(self, offset):
        p = lax.rem(self.place + offset, self.n)
        return remote(
            self.src.at[p], self.dst.at[self.place], self.send_sem.at[p], self.recv_sem.at[self.place], self.device_of(p)
        )

    def start(self):
        @pl.loop(1, self.n)
        def _(offset):
            self._out(offset).start()

        self.dst[self.place] = self.src[self.place]

    def wait_recv(self):
        @pl.loop(1, self.n)
        def _(offset):
            p = lax.rem(self.place + offset, self.n)
            remote(
                self.src.at[p], self.dst.at[p], self.send_sem.at[p], self.recv_sem.at[p], self.device_of(p)
            ).wait_recv()

    def wait_send(self):
        @pl.loop(1, self.n)
        def _(offset):
            self._out(offset).wait_send()


def swap_rows(outer, inner, rows):
    n = outer * inner
    row = lax.broadcasted_iota(jnp.int32, (n, n), 0)
    col = lax.broadcasted_iota(jnp.int32, (n, n), 1)
    matrix = (col == lax.rem(row, outer) * inner + row // outer).astype(BF16)
    return jnp.dot(matrix, rows, preferred_element_type=F32).astype(BF16)


def slot_matrix(routes_ref, live_ref, ndp, capacity):
    count = routes_ref.shape[1]
    target = routes_ref[...]
    row = lax.broadcasted_iota(jnp.int32, (count, count), 0)
    col = lax.broadcasted_iota(jnp.int32, (count, count), 1)
    wide = jnp.broadcast_to(target, (count, count))
    tall = jnp.sum(jnp.where(row == col, wide, 0), axis=1, keepdims=True)
    rank = jnp.sum(((tall == wide) & (row < col)).astype(jnp.int32), axis=0, keepdims=True)
    alive = lax.broadcasted_iota(jnp.int32, (1, count), 1) < live_ref[...]
    slot = jnp.where(alive, rank * ndp + target, -1)
    return (lax.broadcasted_iota(jnp.int32, (ndp * capacity, count), 0) == slot).astype(F32)


def dot_t(left, right):
    return lax.dot_general(left, right, (((1,), (1,)), ((), ())), preferred_element_type=F32)


def t_dot(left, right):
    return lax.dot_general(left, right, (((0,), (0,)), ((), ())), preferred_element_type=F32)


def tiles(total, size, body):
    @pl.loop(0, total // size)
    def _(i):
        body(pl.ds(pl.multiple_of(i * size, size), size))


def kernel(ndp, names, *refs):
    r = SimpleNamespace(**dict(zip(names, refs)))
    me, t = lax.axis_index("dp"), lax.axis_index("tensor")
    nz = ndp // GROUP
    z, j = me // GROUP, lax.rem(me, GROUP)
    y, yx, xl, core = j // 4, j // 2, lax.rem(j // 2, 2), lax.rem(j, 2)
    z_device = lambda p: {"dp": p * GROUP + j}
    j_device = lambda p: {"dp": z * GROUP + p}
    y_device = lambda p: {"dp": z * GROUP + p * 4 + xl * 2 + core}
    x_device = {"dp": me + 2 - 4 * xl}
    sibling = {"dp": me + 1 - 2 * core}
    partner = {"dp": me + 2 - 4 * xl, "tensor": 1 - t}
    width = r.source.shape[1]
    units = r.win.shape[1]
    half = units // 2

    load_in = pltpu.make_async_copy(r.weight_in, r.win, r.load_sem.at[0])
    load_out = pltpu.make_async_copy(r.weight_out, r.wout, r.load_sem.at[1])
    load_in.start()
    load_out.start()

    barrier = pltpu.get_barrier_semaphore()

    @pl.loop(1, nz)
    def _(offset):
        pl.semaphore_signal(barrier, inc=1, device_id=z_device(lax.rem(z + offset, nz)), device_id_type=MESH)

    @pl.loop(1, GROUP)
    def _(offset):
        pl.semaphore_signal(barrier, inc=1, device_id=j_device(lax.rem(j + offset, GROUP)), device_id_type=MESH)

    pl.semaphore_signal(barrier, inc=1, device_id=partner, device_id_type=MESH)

    hot = slot_matrix(r.routes, r.live, ndp, 2)
    r.hot[...] = hot.astype(BF16)
    first = lax.broadcasted_iota(jnp.int32, (ndp, width), 1) == 0

    def outgoing(rank):
        part = hot[rank * ndp : (rank + 1) * ndp]
        empty = jnp.sum(part, axis=1, keepdims=True) < 0.5
        rows = jnp.dot(part.astype(BF16), r.source[...], preferred_element_type=F32)
        return jnp.where(empty & first, ABSENT, rows).astype(BF16)

    def exchanges(prefix):
        bufs = lambda name: tuple(getattr(r, prefix + name + end) for end in ("_out", "_in", "_ss", "_rs"))
        over_z = lambda name: Exchange(nz, z, z_device, bufs(name))
        over_j = lambda name: Exchange(GROUP, j, j_device, bufs(name))
        return over_z("z0"), over_j("j0"), over_j("j1"), over_z("z1")

    z0, j0, j1, z1 = exchanges("a")
    z0.src[...] = outgoing(0).reshape(z0.src.shape)
    j1.src[...] = swap_rows(nz, GROUP, outgoing(1)).reshape(j1.src.shape)
    pl.semaphore_wait(barrier, nz + GROUP - 1)
    z0.start()
    j1.start()

    def across(name, c):
        out, land, ss, rs = (getattr(r, name + end) for end in ("_out", "_in", "_ss", "_rs"))
        return remote(out.at[c], land.at[c], ss.at[c], rs.at[c], partner)

    cot_copy = remote(r.cot, r.cot_in, r.cot_sem.at[0], r.cot_sem.at[1], partner)
    cot_copy.start()
    r.grads[: 2 * ndp] = swap_rows(ndp, 2, r.cot[...])
    load_in.wait()
    load_out.wait()

    def process(k):
        rows = pl.ds(k * ndp, ndp)
        slots = (r.fr_out if k < 2 else r.fr_in)[k % 2].astype(F32)
        present = slots[:, :1] < 0.5 * ABSENT
        frames = jnp.where(present, slots, 0.0)
        centred = frames - jnp.mean(frames, axis=1, keepdims=True)
        inv_std = lax.rsqrt(jnp.mean(centred * centred, axis=1, keepdims=True) + epsilon)
        normed = centred * inv_std
        if k < 2:
            r.normed[k] = normed
            r.inv_std[k] = inv_std
        r.scaled[...] = (normed * r.gain[...]).astype(BF16)
        r.grads[rows] = jnp.where(present, r.grads[rows].astype(F32), 0.0).astype(BF16)

        def tile(n):
            hidden = jnp.dot(r.scaled[...], r.win[:, n], preferred_element_type=F32)
            grad_act = 0.5 * dot_t(r.grads[rows], r.wout[n, :])
            gate = jax.nn.sigmoid(hidden)
            r.act[rows, n] = (hidden * gate).astype(BF16)
            r.gh[rows, n] = (grad_act * gate * (1.0 + hidden * (1.0 - gate))).astype(BF16)

        tiles(units, 512, tile)

    def scaled_grad(k, out, c):
        def tile(n):
            out[c, :, n] = dot_t(r.gh[pl.ds(k * ndp, ndp), :], r.win[n, :]).astype(BF16)

        tiles(width, 512, tile)

    def mix(k, out, c):
        def tile(n):
            out[c, :, n] = jnp.dot(
                r.act[pl.ds(k * ndp, ndp), :], r.wout[:, n], preferred_element_type=F32
            ).astype(BF16)

        tiles(width, 512, tile)

    j1.wait_recv()
    z1.src[...] = swap_rows(GROUP, nz, j1.dst[...].reshape(ndp, width)).reshape(z1.src.shape)
    z1.start()
    z0.wait_recv()
    j0.src[...] = swap_rows(nz, GROUP, z0.dst[...].reshape(ndp, width)).reshape(j0.src.shape)
    j0.start()
    j0.wait_recv()
    r.fr_out[0] = swap_rows(GROUP, nz, j0.dst[...].reshape(ndp, width))
    across("fr", 0).start()
    process(0)
    z1.wait_recv()
    r.fr_out[1] = z1.dst[...].reshape(ndp, width)
    across("fr", 1).start()
    process(1)
    cot_copy.wait_recv()
    r.grads[2 * ndp :] = swap_rows(ndp, 2, r.cot_in[...])
    across("fr", 0).wait_recv()
    process(2)
    scaled_grad(2, r.gs_out, 0)
    across("gs", 0).start()
    across("fr", 1).wait_recv()
    process(3)
    scaled_grad(3, r.gs_out, 1)
    across("gs", 1).start()

    rows_of_z = width // nz
    pair = 2 * rows_of_z
    shape = (2,) + r.mine.shape[1:]

    def product(i, which):
        columns = pl.ds(pl.multiple_of(which * half, half), half)
        left = r.grads[:, pl.ds(pl.multiple_of(i * pair, pair), pair)]
        return (0.5 * t_dot(left, r.act[:, columns])).reshape(shape)

    def to_sibling(i):
        part = pl.ds(2 * i, 2)
        return remote(r.sib_out.at[part], r.sib_in.at[part], r.sib_ss.at[i], r.sib_rs.at[i], sibling)

    @pl.loop(0, nz // 2)
    def _(i):
        r.sib_out[pl.ds(2 * i, 2)] = product(i, 1 - core).astype(BF16)
        to_sibling(i).start()

    @pl.loop(0, nz // 2)
    def _(i):
        r.mine[pl.ds(2 * i, 2)] = product(i, core)

    scaled_grad(0, r.gs_own, 0)
    scaled_grad(1, r.gs_own, 1)

    @pl.loop(0, nz // 2)
    def _(i):
        to_sibling(i).wait_recv()

    up, down, opposite = lax.rem(y + 1, RING), lax.rem(y + 3, RING), lax.rem(y + 2, RING)

    def cores(y_at, x_at):
        p = y_at * 2 + x_at
        return r.mine[:, p] + r.sib_in[:, p].astype(F32)

    def along(name, slot):
        out, land, ss, rs = (getattr(r, name + end) for end in ("_out", "_in", "_ss", "_rs"))
        to_up = slot == 0 if name == "y1" else slot < 2
        return remote(
            out.at[slot], land.at[slot], ss.at[slot], rs.at[slot], y_device(up) if to_up else y_device(down)
        )

    r.y1_out[0] = cores(opposite, 0).astype(BF16)
    along("y1", 0).start()
    r.y1_out[1] = cores(opposite, 1).astype(BF16)
    along("y1", 1).start()
    r.y2_out[1] = cores(up, 1).astype(BF16)
    along("y2", 1).start()
    r.y2_out[2] = cores(down, 0).astype(BF16)
    along("y2", 2).start()
    mix(2, r.mx_out, 0)
    mix(3, r.mx_out, 1)
    along("y1", 0).wait_recv()
    r.y2_out[0] = (cores(up, 0) + r.y1_in[0].astype(F32)).astype(BF16)
    along("y2", 0).start()
    along("y1", 1).wait_recv()
    r.y2_out[3] = (cores(down, 1) + r.y1_in[1].astype(F32)).astype(BF16)
    along("y2", 3).start()

    def gradient(c):
        normed = r.normed[c]
        g = (r.gs_own[c].astype(F32) + r.gs_in[c].astype(F32)) * r.gain[...]
        first_mean = jnp.mean(g, axis=1, keepdims=True)
        second_mean = jnp.mean(g * normed, axis=1, keepdims=True)
        own = r.grads[pl.ds(c * ndp, ndp)].astype(F32)
        return (own + r.inv_std[c] * (g - first_mean - normed * second_mean)).astype(BF16)

    z2, j2, j3, z3 = exchanges("b")
    across("gs", 0).wait_recv()
    z2.src[...] = gradient(0).reshape(z2.src.shape)
    z2.start()
    across("gs", 1).wait_recv()
    j3.src[...] = swap_rows(nz, GROUP, gradient(1)).reshape(j3.src.shape)
    j3.start()
    across("mx", 0).start()
    across("mx", 1).start()
    mix(0, r.mx_own, 0)
    mix(1, r.mx_own, 1)

    for slot in range(4):
        along("y2", slot).wait_recv()
    for x_at in range(2):
        r.total[x_at] = cores(y, x_at) + r.y2_in[x_at].astype(F32) + r.y2_in[2 + x_at].astype(F32)
    r.x_out[...] = r.total[1 - xl].astype(BF16)
    x_copy = remote(r.x_out, r.x_in, r.x_sem.at[0], r.x_sem.at[1], x_device)
    x_copy.start()

    j3.wait_recv()
    z3.src[...] = swap_rows(GROUP, nz, j3.dst[...].reshape(ndp, width)).reshape(z3.src.shape)
    z3.start()
    z2.wait_recv()
    j2.src[...] = swap_rows(nz, GROUP, z2.dst[...].reshape(ndp, width)).reshape(j2.src.shape)
    j2.start()

    x_copy.wait_recv()
    over_z = Exchange(nz, z, z_device, (r.zr_out, r.zr_in, r.zr_ss, r.zr_rs))
    r.zr_out[...] = (r.total[xl] + r.x_in[...].astype(F32)).astype(BF16)
    over_z.start()

    j2.wait_recv()
    given = t_dot(r.hot[:ndp], swap_rows(GROUP, nz, j2.dst[...].reshape(ndp, width)))
    over_z.wait_recv()
    r.last_out[...] = jnp.sum(r.zr_in[...].astype(F32), axis=0)
    last = remote(r.last_out, r.last_in, r.last_sem.at[0], r.last_sem.at[1], sibling)
    last.start()

    for c in range(2):
        across("mx", c).wait_recv()
    mixed_rows = []
    for c in range(2):
        slots = r.fr_out[c].astype(F32)
        frames = jnp.where(slots[:, :1] < 0.5 * ABSENT, slots, 0.0)
        mixed_rows.append((frames + 0.5 * (r.mx_own[c].astype(F32) + r.mx_in[c].astype(F32))).astype(BF16))
    r.mixed[...] = swap_rows(2, ndp, jnp.concatenate(mixed_rows, axis=0))

    z3.wait_recv()
    given += t_dot(r.hot[ndp:], z3.dst[...].reshape(ndp, width))
    r.grad_source[...] = given.astype(BF16)

    last.wait_recv()
    own, other = r.last_out[...], r.last_in[...]
    count = own.shape[0] // 2
    is_low = core == 0
    own = jnp.where(is_low, own[:count], own[count:])
    other = jnp.where(is_low, other[:count], other[count:])
    r.grad_out[:, :half] = jnp.where(is_low, own, other)
    r.grad_out[:, half:] = jnp.where(is_low, other, own)

    last.wait_send()
    x_copy.wait_send()
    cot_copy.wait_send()
    for exchange in (z0, j0, j1, z1, z2, j2, j3, z3, over_z):
        exchange.wait_send()
    for name in ("fr", "gs", "mx"):
        for c in range(2):
            across(name, c).wait_send()
    for slot in range(2):
        along("y1", slot).wait_send()
    for slot in range(4):
        along("y2", slot).wait_send()

    @pl.loop(0, nz // 2)
    def _(i):
        to_sibling(i).wait_send()


def local(source_frames, routes, live_frames, norm_gain, weight_in, weight_out, cotangent):
    ndp = lax.axis_size("dp")
    nz = ndp // GROUP
    width, units = weight_in.shape
    half, strip = units // 2, width // ndp * 2
    vmem = pltpu.VMEM
    inputs = {
        "source": source_frames,
        "routes": routes.reshape(1, -1),
        "live": live_frames.reshape(1, 1),
        "gain": norm_gain.reshape(1, -1),
        "cot": cotangent,
        "weight_in": weight_in,
        "weight_out": weight_out,
    }
    outputs = {
        "mixed": jax.ShapeDtypeStruct(cotangent.shape, BF16),
        "grad_source": jax.ShapeDtypeStruct(source_frames.shape, BF16),
        "grad_out": jax.ShapeDtypeStruct((width // ndp, units), F32),
    }
    scratch = {
        "win": vmem(weight_in.shape, BF16),
        "wout": vmem(weight_out.shape, BF16),
        "load_sem": DMA((2,)),
        "hot": vmem((2 * ndp, source_frames.shape[0]), BF16),
        "cot_in": vmem(cotangent.shape, BF16),
        "cot_sem": DMA((2,)),
        "grads": vmem((4 * ndp, width), BF16),
        "act": vmem((4 * ndp, units), BF16),
        "gh": vmem((4 * ndp, units), BF16),
        "scaled": vmem((ndp, width), BF16),
        "normed": vmem((2, ndp, width), F32),
        "inv_std": vmem((2, ndp, 1), F32),
        "gs_own": vmem((2, ndp, width), BF16),
        "mx_own": vmem((2, ndp, width), BF16),
        "mine": vmem((nz, GROUP // 2, strip, half), F32),
        "total": vmem((2, nz, strip, half), F32),
        "x_out": vmem((nz, strip, half), BF16),
        "x_in": vmem((nz, strip, half), BF16),
        "x_sem": DMA((2,)),
        "last_out": vmem((strip, half), F32),
        "last_in": vmem((strip, half), F32),
        "last_sem": DMA((2,)),
    }

    def both_ways(name, shape, count):
        scratch[name + "_out"] = vmem(shape, BF16)
        scratch[name + "_in"] = vmem(shape, BF16)
        scratch[name + "_ss"] = DMA((count,))
        scratch[name + "_rs"] = DMA((count,))

    for prefix in "ab":
        for c in "01":
            both_ways(prefix + "z" + c, (nz, GROUP, width), nz)
            both_ways(prefix + "j" + c, (GROUP, nz, width), GROUP)
    for name in ("fr", "gs", "mx"):
        both_ways(name, (2, ndp, width), 2)
    both_ways("sib", (nz, GROUP // 2, strip, half), nz // 2)
    both_ways("y1", (2, nz, strip, half), 2)
    both_ways("y2", (4, nz, strip, half), 4)
    both_ways("zr", (nz, strip, half), nz)

    in_vmem = pl.BlockSpec(memory_space=pltpu.VMEM)
    anywhere = pl.BlockSpec(memory_space=pl.ANY)
    mixed, grad_source, grad_out = pl.pallas_call(
        functools.partial(kernel, ndp, list(inputs) + list(outputs) + list(scratch)),
        out_shape=list(outputs.values()),
        in_specs=[anywhere if name.startswith("weight") else in_vmem for name in inputs],
        out_specs=[in_vmem] * 3,
        scratch_shapes=list(scratch.values()),
        compiler_params=pltpu.CompilerParams(
            collective_id=1, has_side_effects=True, vmem_limit_bytes=60 * 1024 * 1024
        ),
        name="module",
    )(*inputs.values())
    return (mixed, grad_source, grad_out.T)


def solution(mesh):
    return jax.shard_map(
        local,
        mesh=mesh,
        in_specs=(
            P(("dp", "tensor"), None),
            P(("dp", "tensor"), None),
            P(("dp", "tensor")),
            P(),
            P(None, "tensor"),
            P("tensor", None),
            P(("dp", "tensor"), None),
        ),
        out_specs=(P(("dp", "tensor"), None), P(("dp", "tensor"), None), P("tensor", "dp")),
        check_vma=False,
    )
```

```python
import functools
from types import SimpleNamespace

import jax
import jax.numpy as jnp
from jax import lax
from jax.experimental import pallas as pl
from jax.experimental.pallas import tpu as pltpu
from jax.sharding import PartitionSpec as P

epsilon = 1e-05
ABSENT = 64.0
MESH = pl.DeviceIdType.MESH
GROUP = 16
RING = 4
DMA = pltpu.SemaphoreType.DMA
BF16, F32 = jnp.bfloat16, jnp.float32


def remote(src, dst, send_sem, recv_sem, device):
    return pltpu.make_async_remote_copy(
        src_ref=src, dst_ref=dst, send_sem=send_sem, recv_sem=recv_sem, device_id=device, device_id_type=MESH
    )


class Exchange:
    def __init__(self, n, place, device_of, buffers):
        self.n, self.place, self.device_of = n, place, device_of
        self.src, self.dst, self.send_sem, self.recv_sem = buffers

    def _out(self, offset):
        p = lax.rem(self.place + offset, self.n)
        return remote(
            self.src.at[p], self.dst.at[self.place], self.send_sem.at[p], self.recv_sem.at[self.place], self.device_of(p)
        )

    def start(self):
        @pl.loop(1, self.n)
        def _(offset):
            self._out(offset).start()

        self.dst[self.place] = self.src[self.place]

    def wait_recv(self):
        @pl.loop(1, self.n)
        def _(offset):
            p = lax.rem(self.place + offset, self.n)
            remote(
                self.src.at[p], self.dst.at[p], self.send_sem.at[p], self.recv_sem.at[p], self.device_of(p)
            ).wait_recv()

    def wait_send(self):
        @pl.loop(1, self.n)
        def _(offset):
            self._out(offset).wait_send()


def picking(source, n):
    return (lax.broadcasted_iota(jnp.int32, (source.shape[0], n), 1) == source).astype(F32).astype(BF16)


def swap_rows(outer, inner, rows):
    n = outer * inner
    row = lax.broadcasted_iota(jnp.int32, (n, 1), 0)
    matrix = picking(lax.rem(row, outer) * inner + row // outer, n)
    return jnp.dot(matrix, rows, preferred_element_type=F32).astype(BF16)


def slot_matrix(routes_ref, live_ref, ndp, capacity):
    count = routes_ref.shape[1]
    row = lax.broadcasted_iota(jnp.int32, (count, count), 0)
    col = lax.broadcasted_iota(jnp.int32, (count, count), 1)
    target = routes_ref[...]
    wide = jnp.broadcast_to(target, (count, count))
    tall = jnp.sum(jnp.where(row == col, wide, 0), axis=1, keepdims=True)
    rank = jnp.sum(((tall == wide) & (row < col)).astype(jnp.int32), axis=0, keepdims=True)
    alive = lax.broadcasted_iota(jnp.int32, (1, count), 1) < live_ref[...]
    slot = jnp.where(alive, rank * ndp + target, -1)
    return (lax.broadcasted_iota(jnp.int32, (ndp * capacity, count), 0) == slot).astype(F32)


def dot_t(left, right):
    return lax.dot_general(left, right, (((1,), (1,)), ((), ())), preferred_element_type=F32)


def t_dot(left, right):
    return lax.dot_general(left, right, (((0,), (0,)), ((), ())), preferred_element_type=F32)


def tiles(total, size, body, start=0):
    @pl.loop(0, total // size)
    def _(i):
        body(pl.ds(pl.multiple_of(start + i * size, size), size))


class Route:
    def __init__(self, z_first, over_z, over_j):
        self.z_first = z_first
        self.nz, self.nj = over_z.n, over_j.n
        self.first, self.second = (over_z, over_j) if z_first else (over_j, over_z)

    def _send(self, exchange, rows):
        exchange.src[...] = rows.reshape(exchange.src.shape)
        exchange.start()

    def _got(self, exchange):
        exchange.wait_recv()
        shape = exchange.dst.shape
        return exchange.dst[...].reshape(shape[0] * shape[1], shape[2])

    def start(self, rows):
        self._send(self.first, rows if self.z_first else swap_rows(self.nz, self.nj, rows))

    def middle(self):
        a, b = (self.nz, self.nj) if self.z_first else (self.nj, self.nz)
        self._send(self.second, swap_rows(a, b, self._got(self.first)))

    def finish(self):
        rows = self._got(self.second)
        return swap_rows(self.nj, self.nz, rows) if self.z_first else rows

    def wait_send(self):
        self.first.wait_send()
        self.second.wait_send()


def kernel(ndp, names, *refs):
    r = SimpleNamespace(**dict(zip(names, refs)))
    me, t = lax.axis_index("dp"), lax.axis_index("tensor")
    nz = ndp // GROUP
    z, j = me // GROUP, lax.rem(me, GROUP)
    y, xl, core = j // 4, lax.rem(j // 2, 2), lax.rem(j, 2)
    z_device = lambda p: {"dp": p * GROUP + j}
    j_device = lambda p: {"dp": z * GROUP + p}
    y_device = lambda p: {"dp": z * GROUP + p * 4 + xl * 2 + core}
    x_device = {"dp": me + 2 - 4 * xl}
    sibling = {"dp": me + 1 - 2 * core}
    partner = {"dp": me + 2 - 4 * xl, "tensor": 1 - t}
    width = r.source.shape[1]
    units = r.win.shape[1]
    half = units // 2
    wide = width // 2
    halves = [slice(0, wide), slice(wide, width)]

    load_cot = pltpu.make_async_copy(r.cotangent, r.cot, r.load_sem.at[2])
    load_in = pltpu.make_async_copy(r.weight_in, r.win, r.load_sem.at[0])
    load_out = pltpu.make_async_copy(r.weight_out, r.wout, r.load_sem.at[1])
    load_cot.start()
    load_in.start()
    load_out.start()

    barrier = pltpu.get_barrier_semaphore()

    @pl.loop(1, nz)
    def _(offset):
        pl.semaphore_signal(barrier, inc=1, device_id=z_device(lax.rem(z + offset, nz)), device_id_type=MESH)

    @pl.loop(1, GROUP)
    def _(offset):
        pl.semaphore_signal(barrier, inc=1, device_id=j_device(lax.rem(j + offset, GROUP)), device_id_type=MESH)

    pl.semaphore_signal(barrier, inc=1, device_id=partner, device_id_type=MESH)

    def exchange(name, n, place, device_of):
        return Exchange(n, place, device_of, tuple(getattr(r, name + end) for end in ("_out", "_in", "_ss", "_rs")))

    def routed(name, z_first):
        return Route(z_first, exchange(name + "z", nz, z, z_device), exchange(name + "j", GROUP, j, j_device))

    def one_way(name, slot, device, part=None):
        out, land, ss, rs = (getattr(r, name + end) for end in ("_out", "_in", "_ss", "_rs"))
        index, sem = (slot, slot) if part is None else ((slot, slice(None), halves[part]), 2 * slot + part)
        return remote(out.at[index], land.at[index], ss.at[sem], rs.at[sem], device)

    r.gain_row[...] = r.gain[...].reshape(1, -1)
    hot = slot_matrix(r.routes, r.live, ndp, 2)
    r.hot[...] = hot.astype(BF16)
    first = lax.broadcasted_iota(jnp.int32, (ndp, width), 1) == 0

    def outgoing(rank):
        part = hot[rank * ndp : (rank + 1) * ndp]
        empty = jnp.sum(part, axis=1, keepdims=True) < 0.5
        rows = jnp.dot(part.astype(BF16), r.source[...], preferred_element_type=F32)
        return jnp.where(empty & first, ABSENT, rows).astype(BF16)

    there = [routed("a" + str(i), i == 0) for i in range(4)]
    leaving = outgoing(0)
    pl.semaphore_wait(barrier, nz + GROUP - 1)
    there[0].start(leaving[:, halves[0]])
    there[1].start(leaving[:, halves[1]])
    load_cot.wait()
    cot_copy = remote(r.cot, r.cot_in, r.cot_sem.at[0], r.cot_sem.at[1], partner)
    cot_copy.start()
    leaving = outgoing(1)
    there[2].start(leaving[:, halves[0]])
    there[3].start(leaving[:, halves[1]])

    strip = width // (nz * 8)
    step = width // RING

    def turn(side, rows):
        @pl.loop(0, RING)
        def _(i):
            row = lax.broadcasted_iota(jnp.int32, (step, 1), 0)
            x_at, z_at, rest = row // (step // 2), lax.rem(row // strip, nz), lax.rem(row, strip)
            pick = picking((z_at * 8 + i * 2 + x_at) * strip + rest, width)
            at = pl.ds(pl.multiple_of(i * step, step), step)
            r.turned[at, side * 2 * ndp : (side + 1) * 2 * ndp] = dot_t(pick, rows).astype(BF16)

    def order_cot(side, rows):
        rows = swap_rows(ndp, 2, rows)
        r.cots[side * 2 * ndp : (side + 1) * 2 * ndp] = rows
        turn(side, rows)

    order_cot(0, r.cot[...])
    there[1].middle()
    there[0].middle()
    load_in.wait()
    load_out.wait()

    def process(k):
        c = k % 2
        rows = pl.ds(k * ndp, ndp)
        slots = (r.fr_out if k < 2 else r.fr_in)[c].astype(F32)
        present = slots[:, :1] < 0.5 * ABSENT
        frames = jnp.where(present, slots, 0.0)
        centred = frames - jnp.mean(frames, axis=1, keepdims=True)
        inv_std = lax.rsqrt(jnp.mean(centred * centred, axis=1, keepdims=True) + epsilon)
        normed = centred * inv_std
        if k < 2:
            r.normed[c] = normed
            r.inv_std[c] = inv_std
        r.scaled[...] = (normed * r.gain_row[...]).astype(BF16)
        r.grads[rows] = jnp.where(present, r.cots[rows].astype(F32), 0.0).astype(BF16)

        def tile(n):
            hidden = jnp.dot(r.scaled[...], r.win[:, n], preferred_element_type=F32)
            grad_act = 0.5 * dot_t(r.grads[rows], r.wout[n, :])
            gate = jax.nn.sigmoid(hidden)
            r.act[rows, n] = jnp.where(present, hidden * gate, 0.0).astype(BF16)
            r.gh[rows, n] = (grad_act * gate * (1.0 + hidden * (1.0 - gate))).astype(BF16)

        tiles(units, 512, tile)

    def scaled_grad(k, out, c, start=0, length=None):
        def tile(n):
            out[c, :, n] = dot_t(r.gh[pl.ds(k * ndp, ndp), :], r.win[n, :]).astype(BF16)

        tiles(length or width, 384, tile, start)

    def mix(k, out, c):
        def tile(n):
            out[c, :, n] = jnp.dot(
                r.act[pl.ds(k * ndp, ndp), :], r.wout[:, n], preferred_element_type=F32
            ).astype(BF16)

        tiles(width, 512, tile)

    frames_over = [one_way("fr", i // 2, partner, i % 2) for i in range(4)]

    def land(i):
        r.fr_out[i // 2, :, halves[i % 2]] = there[i].finish()
        frames_over[i].start()

    there[2].middle()
    land(0)
    land(1)
    there[3].middle()
    process(0)
    scaled_grad(0, r.gs_own, 0)
    cot_copy.wait_recv()
    order_cot(1, r.cot_in[...])
    land(2)
    land(3)
    frames_over[0].wait_recv()
    frames_over[1].wait_recv()
    process(2)
    sums = [one_way("gs", i // 2, partner, i % 2) for i in range(4)]

    def send_sums(c):
        for part in range(2):
            scaled_grad(2 + c, r.gs_out, c, part * wide, wide)
            sums[2 * c + part].start()

    send_sums(0)
    process(1)
    scaled_grad(1, r.gs_own, 1)
    frames_over[2].wait_recv()
    frames_over[3].wait_recv()
    process(3)
    send_sums(1)

    up, down, opposite = lax.rem(y + 1, RING), lax.rem(y + 3, RING), lax.rem(y + 2, RING)
    order = [opposite, up, down, y]

    def product(y_at, which):
        columns = pl.ds(pl.multiple_of(which * half, half), half)
        left = r.turned[pl.ds(pl.multiple_of(y_at * step, step), step), :]
        return (0.5 * jnp.dot(left, r.act[:, columns], preferred_element_type=F32)).reshape(2, step // 2, half)

    def to_sibling(i):
        part = pl.ds(2 * order[i], 2)
        return remote(r.sib_out.at[part], r.sib_in.at[part], r.sib_ss.at[i], r.sib_rs.at[i], sibling)

    for i in range(4):
        r.sib_out[pl.ds(2 * order[i], 2)] = product(order[i], 1 - core).astype(BF16)
        to_sibling(i).start()

    def keep(i):
        r.mine[pl.ds(2 * order[i], 2)] = product(order[i], core)
        to_sibling(i).wait_recv()

    block = half // 2
    blocks = [slice(0, block), slice(block, half)]
    part_rows = step // 4

    def cores(y_at, x_at, b):
        p = y_at * 2 + x_at
        return r.mine[p, :, blocks[b]] + r.sib_in[p, :, blocks[b]].astype(F32)

    def ring1(name, slot):
        return one_way(name, slot, y_device(down) if slot else y_device(up))

    def ring2(name, slot):
        return one_way(name, slot, y_device(down) if slot // 2 else y_device(up))

    def send(copy, buffer, index, value):
        buffer[index] = value.astype(BF16)
        copy.start()

    def x_first(i):
        return remote(r.bx_out.at[i], r.bx_in.at[i], r.bx_ss.at[i], r.bx_rs.at[i], x_device)

    keep(0)
    for s in range(2):
        send(ring1("a1", s), r.a1_out, s, cores(opposite, s, 0))
    send(x_first(0), r.bx_out, 0, cores(opposite, 1 - xl, 1))
    keep(1)
    send(ring2("a2", 1), r.a2_out, 1, cores(up, 1, 0))
    send(x_first(1), r.bx_out, 1, cores(up, 1 - xl, 1))
    keep(2)
    send(ring2("a2", 2), r.a2_out, 2, cores(down, 0, 0))
    send(x_first(2), r.bx_out, 2, cores(down, 1 - xl, 1))
    keep(3)
    send(x_first(3), r.bx_out, 3, cores(y, 1 - xl, 1))

    def gradient(c):
        normed = r.normed[c]
        g = (r.gs_own[c].astype(F32) + r.gs_in[c].astype(F32)) * r.gain_row[...]
        first_mean = jnp.mean(g, axis=1, keepdims=True)
        second_mean = jnp.mean(g * normed, axis=1, keepdims=True)
        own = r.grads[pl.ds(c * ndp, ndp)].astype(F32)
        return (own + r.inv_std[c] * (g - first_mean - normed * second_mean)).astype(BF16)

    back = [routed("b" + str(i), i % 2 == 0) for i in range(4)]

    def give(c):
        sums[2 * c].wait_recv()
        sums[2 * c + 1].wait_recv()
        rows = gradient(c)
        back[2 * c].start(rows[:, halves[0]])
        back[2 * c + 1].start(rows[:, halves[1]])

    give(0)
    mix(2, r.mx_out, 0)
    mix(3, r.mx_out, 1)
    ring1("a1", 0).wait_recv()
    send(ring2("a2", 0), r.a2_out, 0, cores(up, 0, 0) + r.a1_in[0].astype(F32))
    ring1("a1", 1).wait_recv()
    send(ring2("a2", 3), r.a2_out, 3, cores(down, 1, 0) + r.a1_in[1].astype(F32))

    def summed(i):
        r.bsum[i] = cores(order[i], xl, 1) + r.bx_in[i].astype(F32)

    x_first(0).wait_recv()
    summed(0)
    for s in range(2):
        send(ring1("b1", s), r.b1_out, s, r.bsum[0, s * part_rows : (s + 1) * part_rows])
    back[1].middle()
    x_first(1).wait_recv()
    summed(1)
    send(ring2("b2", 1), r.b2_out, 1, r.bsum[1, part_rows:])
    x_first(2).wait_recv()
    summed(2)
    send(ring2("b2", 2), r.b2_out, 2, r.bsum[2, :part_rows])
    give(1)
    mixes = [one_way("mx", c, partner) for c in range(2)]
    mixes[0].start()
    mixes[1].start()
    back[0].middle()
    ring1("b1", 0).wait_recv()
    send(ring2("b2", 0), r.b2_out, 0, r.bsum[1, :part_rows] + r.b1_in[0].astype(F32))
    ring1("b1", 1).wait_recv()
    send(ring2("b2", 3), r.b2_out, 3, r.bsum[2, part_rows:] + r.b1_in[1].astype(F32))
    mix(0, r.mx_own, 0)
    mix(1, r.mx_own, 1)
    for slot in range(4):
        ring2("a2", slot).wait_recv()
    for s in range(2):
        r.total[s] = cores(y, s, 0) + r.a2_in[s].astype(F32) + r.a2_in[2 + s].astype(F32)
    r.ax_out[...] = r.total[1 - xl].astype(BF16)
    x_last = remote(r.ax_out, r.ax_in, r.ax_ss.at[0], r.ax_rs.at[0], x_device)
    x_last.start()
    back[3].middle()
    back[2].middle()
    x_first(3).wait_recv()
    summed(3)
    for slot in range(4):
        ring2("b2", slot).wait_recv()
    over_z = [exchange("s" + str(b), nz, z, z_device) for b in range(2)]
    for s in range(2):
        at = slice(s * part_rows, (s + 1) * part_rows)
        r.bsum[3, at] = r.bsum[3, at] + r.b2_in[s].astype(F32) + r.b2_in[2 + s].astype(F32)
    r.s1_out[...] = r.bsum[3].astype(BF16).reshape(r.s1_out.shape)
    over_z[1].start()
    x_last.wait_recv()
    r.s0_out[...] = (r.total[xl] + r.ax_in[...].astype(F32)).astype(BF16).reshape(r.s0_out.shape)
    over_z[0].start()

    r.rows[0, :, halves[0]] = back[0].finish()
    r.rows[0, :, halves[1]] = back[1].finish()
    for c in range(2):
        mixes[c].wait_recv()
    mixed_rows = []
    for c in range(2):
        slots = r.fr_out[c].astype(F32)
        frames = jnp.where(slots[:, :1] < 0.5 * ABSENT, slots, 0.0)
        mixed_rows.append((frames + 0.5 * (r.mx_own[c].astype(F32) + r.mx_in[c].astype(F32))).astype(BF16))
    r.mixed[...] = swap_rows(2, ndp, jnp.concatenate(mixed_rows, axis=0))
    for b in (1, 0):
        over_z[b].wait_recv()
        r.last_out[:, blocks[b]] = jnp.sum((r.s0_in, r.s1_in)[b][...].astype(F32), axis=0)
    last = remote(r.last_out, r.last_in, r.last_sem.at[0], r.last_sem.at[1], sibling)
    last.start()
    r.rows[1, :, halves[1]] = back[3].finish()
    r.rows[1, :, halves[0]] = back[2].finish()
    r.grad_source[...] = (t_dot(r.hot[:ndp], r.rows[0]) + t_dot(r.hot[ndp:], r.rows[1])).astype(BF16)

    last.wait_recv()
    own, other = r.last_out[...], r.last_in[...]
    count = own.shape[0] // 2
    is_low = core == 0
    own = jnp.where(is_low, own[:count], own[count:])
    other = jnp.where(is_low, other[:count], other[count:])
    r.grad_out[:, :half] = jnp.where(is_low, own, other)
    r.grad_out[:, half:] = jnp.where(is_low, other, own)

    last.wait_send()
    cot_copy.wait_send()
    x_last.wait_send()
    for copy in sums + mixes + frames_over + there + back + over_z:
        copy.wait_send()
    for name in ("a", "b"):
        for slot in range(2):
            ring1(name + "1", slot).wait_send()
        for slot in range(4):
            ring2(name + "2", slot).wait_send()
    for i in range(4):
        to_sibling(i).wait_send()
        x_first(i).wait_send()


def finish_kernel(mixed, grad_source, grad_out, mixed_out, grad_source_out, grad_out_out):
    mixed_out[...] = mixed[...]
    grad_source_out[...] = grad_source[...]
    grad_out_out[...] = grad_out[...]


def local(source_frames, routes, live_frames, norm_gain, weight_in, weight_out, cotangent):
    ndp = lax.axis_size("dp")
    nz = ndp // GROUP
    width, units = weight_in.shape
    half, strip = units // 2, width // ndp * 2
    block, tall = half // 2, width // 8
    vmem = pltpu.VMEM
    inputs = {
        "source": source_frames,
        "routes": routes.reshape(1, -1),
        "live": live_frames.reshape(1, 1),
        "gain": norm_gain,
        "cotangent": cotangent,
        "weight_in": weight_in,
        "weight_out": weight_out,
    }
    outputs = {
        "mixed": jax.ShapeDtypeStruct(cotangent.shape, BF16),
        "grad_source": jax.ShapeDtypeStruct(source_frames.shape, BF16),
        "grad_out": jax.ShapeDtypeStruct((width // ndp, units), F32),
    }
    scratch = {
        "win": vmem(weight_in.shape, BF16),
        "wout": vmem(weight_out.shape, BF16),
        "cot": vmem(cotangent.shape, BF16),
        "cot_in": vmem(cotangent.shape, BF16),
        "cot_sem": DMA((2,)),
        "cots": vmem((4 * ndp, width), BF16),
        "load_sem": DMA((3,)),
        "hot": vmem((2 * ndp, source_frames.shape[0]), BF16),
        "turned": vmem((width, 4 * ndp), BF16),
        "grads": vmem((4 * ndp, width), BF16),
        "act": vmem((4 * ndp, units), BF16),
        "gh": vmem((4 * ndp, units), BF16),
        "gain_row": vmem((1, width), F32),
        "scaled": vmem((ndp, width), BF16),
        "normed": vmem((2, ndp, width), F32),
        "inv_std": vmem((2, ndp, 1), F32),
        "gs_own": vmem((2, ndp, width), BF16),
        "mx_own": vmem((2, ndp, width), BF16),
        "rows": vmem((2, ndp, width), BF16),
        "mine": vmem((8, tall, half), F32),
        "total": vmem((2, tall, block), F32),
        "bsum": vmem((4, tall, block), F32),
        "last_out": vmem((strip, half), F32),
        "last_in": vmem((strip, half), F32),
        "last_sem": DMA((2,)),
    }

    def both_ways(name, shape, count):
        scratch[name + "_out"] = vmem(shape, BF16)
        scratch[name + "_in"] = vmem(shape, BF16)
        scratch[name + "_ss"] = DMA((count,))
        scratch[name + "_rs"] = DMA((count,))

    for prefix in "ab":
        for i in "0123":
            both_ways(prefix + i + "z", (nz, GROUP, width // 2), nz)
            both_ways(prefix + i + "j", (GROUP, nz, width // 2), GROUP)
    for name, count in (("fr", 4), ("gs", 4), ("mx", 2)):
        both_ways(name, (2, ndp, width), count)
    both_ways("sib", (8, tall, half), 4)
    both_ways("a1", (2, tall, block), 2)
    both_ways("a2", (4, tall, block), 4)
    both_ways("b1", (2, tall // 2, block), 2)
    both_ways("b2", (4, tall // 2, block), 4)
    both_ways("ax", (tall, block), 1)
    both_ways("bx", (4, tall, block), 4)
    both_ways("s0", (nz, strip, block), nz)
    both_ways("s1", (nz, strip, block), nz)

    in_vmem = pl.BlockSpec(memory_space=pltpu.VMEM)
    anywhere = pl.BlockSpec(memory_space=pl.ANY)
    from_hbm = ("weight_in", "weight_out", "cotangent")
    results = pl.pallas_call(
        functools.partial(kernel, ndp, list(inputs) + list(outputs) + list(scratch)),
        out_shape=list(outputs.values()),
        in_specs=[anywhere if name in from_hbm else in_vmem for name in inputs],
        out_specs=[in_vmem] * 3,
        scratch_shapes=list(scratch.values()),
        compiler_params=pltpu.CompilerParams(
            collective_id=1, has_side_effects=True, vmem_limit_bytes=60 * 1024 * 1024
        ),
        name="module",
    )(*inputs.values())
    mixed, grad_source, grad_out = pl.pallas_call(
        finish_kernel,
        out_shape=list(outputs.values()),
        in_specs=[in_vmem] * 3,
        out_specs=[in_vmem] * 3,
        name="finish",
    )(*results)
    return (mixed, grad_source, grad_out.T)


def solution(mesh):
    return jax.shard_map(
        local,
        mesh=mesh,
        in_specs=(
            P(("dp", "tensor"), None),
            P(("dp", "tensor"), None),
            P(("dp", "tensor")),
            P(),
            P(None, "tensor"),
            P("tensor", None),
            P(("dp", "tensor"), None),
        ),
        out_specs=(P(("dp", "tensor"), None), P(("dp", "tensor"), None), P("tensor", "dp")),
        check_vma=False,
    )
```

```python
import functools
from types import SimpleNamespace

import jax
import jax.numpy as jnp
from jax import lax
from jax.experimental import pallas as pl
from jax.experimental.pallas import tpu as pltpu
from jax.sharding import PartitionSpec as P

epsilon = 1e-05
ABSENT = 64.0
MESH = pl.DeviceIdType.MESH
GROUP = 16
RING = 4
DMA = pltpu.SemaphoreType.DMA
BF16, F32 = jnp.bfloat16, jnp.float32


def remote(src, dst, send_sem, recv_sem, device):
    return pltpu.make_async_remote_copy(
        src_ref=src, dst_ref=dst, send_sem=send_sem, recv_sem=recv_sem, device_id=device, device_id_type=MESH
    )


class Exchange:
    def __init__(self, n, place, device_of, buffers):
        self.n, self.place, self.device_of = n, place, device_of
        self.src, self.dst, self.send_sem, self.recv_sem = buffers

    def start(self):
        @pl.loop(1, self.n)
        def _(offset):
            p = (self.place + offset) & (self.n - 1)
            remote(
                self.src.at[p], self.dst.at[self.place], self.send_sem.at[0], self.recv_sem.at[0], self.device_of(p)
            ).start()

        self.dst[self.place] = self.src[self.place]

    def _all(self):
        part = pl.ds(0, self.n - 1)
        p = (self.place + 1) & (self.n - 1)
        return remote(self.src.at[part], self.dst.at[part], self.send_sem.at[0], self.recv_sem.at[0], self.device_of(p))

    def wait_recv(self):
        self._all().wait_recv()

    def wait_send(self):
        self._all().wait_send()


def picking(source, n):
    return (lax.broadcasted_iota(jnp.int32, (source.shape[0], n), 1) == source).astype(F32).astype(BF16)


def swap_rows(outer, inner, rows):
    n = outer * inner
    row = lax.broadcasted_iota(jnp.int32, (n, 1), 0)
    matrix = picking(lax.rem(row, outer) * inner + row // outer, n)
    return jnp.dot(matrix, rows, preferred_element_type=F32).astype(BF16)


def slot_matrix(routes_ref, live_ref, ndp, capacity):
    count = routes_ref.shape[1]
    row = lax.broadcasted_iota(jnp.int32, (count, count), 0)
    col = lax.broadcasted_iota(jnp.int32, (count, count), 1)
    target = routes_ref[...]
    wide = jnp.broadcast_to(target, (count, count))
    tall = jnp.sum(jnp.where(row == col, wide, 0), axis=1, keepdims=True)
    rank = jnp.sum(((tall == wide) & (row < col)).astype(jnp.int32), axis=0, keepdims=True)
    alive = lax.broadcasted_iota(jnp.int32, (1, count), 1) < live_ref[...]
    slot = jnp.where(alive, rank * ndp + target, -1)
    return (lax.broadcasted_iota(jnp.int32, (ndp * capacity, count), 0) == slot).astype(F32)


def dot_t(left, right):
    return lax.dot_general(left, right, (((1,), (1,)), ((), ())), preferred_element_type=F32)


def t_dot(left, right):
    return lax.dot_general(left, right, (((0,), (0,)), ((), ())), preferred_element_type=F32)


def tiles(total, size, body, start=0):
    @pl.loop(0, total // size)
    def _(i):
        body(pl.ds(pl.multiple_of(start + i * size, size), size))


class Route:
    def __init__(self, z_first, over_z, over_j):
        self.z_first = z_first
        self.nz, self.nj = over_z.n, over_j.n
        self.first, self.second = (over_z, over_j) if z_first else (over_j, over_z)

    def _send(self, exchange, rows):
        exchange.src[...] = rows.reshape(exchange.src.shape)
        exchange.start()

    def _got(self, exchange):
        exchange.wait_recv()
        shape = exchange.dst.shape
        return exchange.dst[...].reshape(shape[0] * shape[1], shape[2])

    def start(self, rows):
        self._send(self.first, rows if self.z_first else swap_rows(self.nz, self.nj, rows))

    def middle(self):
        a, b = (self.nz, self.nj) if self.z_first else (self.nj, self.nz)
        self._send(self.second, swap_rows(a, b, self._got(self.first)))

    def finish(self):
        rows = self._got(self.second)
        return swap_rows(self.nj, self.nz, rows) if self.z_first else rows

    def wait_send(self):
        self.first.wait_send()
        self.second.wait_send()


def kernel(ndp, names, *refs):
    r = SimpleNamespace(**dict(zip(names, refs)))
    me, t = lax.axis_index("dp"), lax.axis_index("tensor")
    nz = ndp // GROUP
    z, j = me // GROUP, lax.rem(me, GROUP)
    y, xl, core = j // 4, lax.rem(j // 2, 2), lax.rem(j, 2)
    z_device = lambda p: {"dp": p * GROUP + j}
    j_device = lambda p: {"dp": z * GROUP + p}
    y_device = lambda p: {"dp": z * GROUP + p * 4 + xl * 2 + core}
    x_device = {"dp": me + 2 - 4 * xl}
    sibling = {"dp": me + 1 - 2 * core}
    partner = {"dp": me + 2 - 4 * xl, "tensor": 1 - t}
    width = r.source.shape[1]
    units = r.win.shape[1]
    half = units // 2
    wide = width // 2
    halves = [slice(0, wide), slice(wide, width)]

    load_cot = pltpu.make_async_copy(r.cotangent, r.cot, r.load_sem.at[2])
    load_in = pltpu.make_async_copy(r.weight_in, r.win, r.load_sem.at[0])
    load_out = pltpu.make_async_copy(r.weight_out, r.wout, r.load_sem.at[1])
    load_cot.start()
    load_in.start()
    load_out.start()

    barrier = pltpu.get_barrier_semaphore()

    @pl.loop(1, nz)
    def _(offset):
        pl.semaphore_signal(barrier, inc=1, device_id=z_device(lax.rem(z + offset, nz)), device_id_type=MESH)

    @pl.loop(1, GROUP)
    def _(offset):
        pl.semaphore_signal(barrier, inc=1, device_id=j_device(lax.rem(j + offset, GROUP)), device_id_type=MESH)

    pl.semaphore_signal(barrier, inc=1, device_id=partner, device_id_type=MESH)

    def exchange(name, n, place, device_of):
        return Exchange(n, place, device_of, tuple(getattr(r, name + end) for end in ("_out", "_in", "_ss", "_rs")))

    def routed(name, z_first):
        return Route(z_first, exchange(name + "z", nz, z, z_device), exchange(name + "j", GROUP, j, j_device))

    def one_way(name, slot, device, part=None):
        out, land, ss, rs = (getattr(r, name + end) for end in ("_out", "_in", "_ss", "_rs"))
        index, sem = (slot, slot) if part is None else ((slot, slice(None), halves[part]), 2 * slot + part)
        return remote(out.at[index], land.at[index], ss.at[sem], rs.at[sem], device)

    r.gain_row[...] = r.gain[...].reshape(1, -1)
    hot = slot_matrix(r.routes, r.live, ndp, 2)
    r.hot[...] = hot.astype(BF16)
    first = lax.broadcasted_iota(jnp.int32, (ndp, width), 1) == 0

    def outgoing(rank):
        part = hot[rank * ndp : (rank + 1) * ndp]
        empty = jnp.sum(part, axis=1, keepdims=True) < 0.5
        rows = jnp.dot(part.astype(BF16), r.source[...], preferred_element_type=F32)
        return jnp.where(empty & first, ABSENT, rows).astype(BF16)

    there = [routed("a" + str(i), i < 2) for i in range(4)]
    leaving = outgoing(0)
    pl.semaphore_wait(barrier, nz + GROUP - 1)
    there[0].start(leaving[:, halves[0]])
    there[1].start(leaving[:, halves[1]])
    load_cot.wait()
    cot_copy = remote(r.cot, r.cot_in, r.cot_sem.at[0], r.cot_sem.at[1], partner)
    cot_copy.start()
    leaving = outgoing(1)
    there[2].start(leaving[:, halves[0]])
    there[3].start(leaving[:, halves[1]])

    strip = width // (nz * 8)
    step = width // RING

    def turn(side, rows):
        @pl.loop(0, RING)
        def _(i):
            row = lax.broadcasted_iota(jnp.int32, (step, 1), 0)
            x_at, z_at, rest = row // (step // 2), lax.rem(row // strip, nz), lax.rem(row, strip)
            pick = picking((z_at * 8 + i * 2 + x_at) * strip + rest, width)
            at = pl.ds(pl.multiple_of(i * step, step), step)
            r.turned[at, side * 2 * ndp : (side + 1) * 2 * ndp] = dot_t(pick, rows).astype(BF16)

    def order_cot(side, rows):
        rows = swap_rows(ndp, 2, rows)
        r.cots[side * 2 * ndp : (side + 1) * 2 * ndp] = rows
        turn(side, rows)

    order_cot(0, r.cot[...])
    there[0].middle()
    there[2].middle()
    load_in.wait()
    load_out.wait()

    def process(k):
        c = k % 2
        rows = pl.ds(k * ndp, ndp)
        slots = (r.fr_out if k < 2 else r.fr_in)[c].astype(F32)
        present = slots[:, :1] < 0.5 * ABSENT
        frames = jnp.where(present, slots, 0.0)
        centred = frames - jnp.mean(frames, axis=1, keepdims=True)
        inv_std = lax.rsqrt(jnp.mean(centred * centred, axis=1, keepdims=True) + epsilon)
        normed = centred * inv_std
        if k < 2:
            r.normed[c] = normed
            r.inv_std[c] = inv_std
        r.scaled[...] = (normed * r.gain_row[...]).astype(BF16)
        r.grads[rows] = jnp.where(present, r.cots[rows].astype(F32), 0.0).astype(BF16)

        def tile(n):
            hidden = jnp.dot(r.scaled[...], r.win[:, n], preferred_element_type=F32)
            grad_act = 0.5 * dot_t(r.grads[rows], r.wout[n, :])
            gate = jax.nn.sigmoid(hidden)
            r.act[rows, n] = jnp.where(present, hidden * gate, 0.0).astype(BF16)
            r.gh[rows, n] = (grad_act * gate * (1.0 + hidden * (1.0 - gate))).astype(BF16)

        tiles(units, 512, tile)

    def scaled_grad(k, out, c, start=0, length=None):
        def tile(n):
            out[c, :, n] = dot_t(r.gh[pl.ds(k * ndp, ndp), :], r.win[n, :]).astype(BF16)

        tiles(length or width, 384, tile, start)

    def mix(k, out, c):
        def tile(n):
            out[c, :, n] = jnp.dot(
                r.act[pl.ds(k * ndp, ndp), :], r.wout[:, n], preferred_element_type=F32
            ).astype(BF16)

        tiles(width, 512, tile)

    frames_over = [one_way("fr", i // 2, partner, i % 2) for i in range(4)]

    def land(i):
        r.fr_out[i // 2, :, halves[i % 2]] = there[i].finish()
        frames_over[i].start()

    there[1].middle()
    land(0)
    there[3].middle()
    land(1)
    process(0)
    scaled_grad(0, r.gs_own, 0)
    cot_copy.wait_recv()
    order_cot(1, r.cot_in[...])
    land(2)
    land(3)
    mix(0, r.mx_own, 0)
    frames_over[0].wait_recv()
    frames_over[1].wait_recv()
    process(2)
    sums = [one_way("gs", i // 2, partner, i % 2) for i in range(4)]

    def send_sums(c):
        for part in range(2):
            scaled_grad(2 + c, r.gs_out, c, part * wide, wide)
            sums[2 * c + part].start()

    send_sums(0)
    process(1)
    scaled_grad(1, r.gs_own, 1)
    for route in there:
        route.wait_send()
    frames_over[2].wait_recv()
    frames_over[3].wait_recv()
    process(3)
    send_sums(1)

    up, down, opposite = lax.rem(y + 1, RING), lax.rem(y + 3, RING), lax.rem(y + 2, RING)
    order = [opposite, up, down, y]

    def product(y_at, which):
        columns = pl.ds(pl.multiple_of(which * half, half), half)
        left = r.turned[pl.ds(pl.multiple_of(y_at * step, step), step), :]
        return (0.5 * jnp.dot(left, r.act[:, columns], preferred_element_type=F32)).reshape(2, step // 2, half)

    def to_sibling(i):
        part = pl.ds(2 * order[i], 2)
        return remote(r.sib_out.at[part], r.sib_in.at[part], r.sib_ss.at[i], r.sib_rs.at[i], sibling)

    for i in range(4):
        r.sib_out[pl.ds(2 * order[i], 2)] = product(order[i], 1 - core).astype(BF16)
        to_sibling(i).start()

    def keep(i):
        r.mine[pl.ds(2 * order[i], 2)] = product(order[i], core)
        to_sibling(i).wait_recv()

    block = half // 2
    blocks = [slice(0, block), slice(block, half)]
    part_rows = step // 4

    def cores(y_at, x_at, b):
        p = y_at * 2 + x_at
        return r.mine[p, :, blocks[b]] + r.sib_in[p, :, blocks[b]].astype(F32)

    def ring1(name, slot):
        return one_way(name, slot, y_device(down) if slot else y_device(up))

    def ring2(name, slot):
        return one_way(name, slot, y_device(down) if slot // 2 else y_device(up))

    def send(copy, buffer, index, value):
        buffer[index] = value.astype(BF16)
        copy.start()

    def x_first(i):
        return remote(r.bx_out.at[i], r.bx_in.at[i], r.bx_ss.at[i], r.bx_rs.at[i], x_device)

    keep(0)
    send(x_first(0), r.bx_out, 0, cores(opposite, 1 - xl, 1))
    for s in range(2):
        send(ring1("a1", s), r.a1_out, s, cores(opposite, s, 0))
    keep(1)
    send(x_first(1), r.bx_out, 1, cores(up, 1 - xl, 1))
    send(ring2("a2", 1), r.a2_out, 1, cores(up, 1, 0))
    keep(2)
    send(x_first(2), r.bx_out, 2, cores(down, 1 - xl, 1))
    send(ring2("a2", 2), r.a2_out, 2, cores(down, 0, 0))
    keep(3)
    send(x_first(3), r.bx_out, 3, cores(y, 1 - xl, 1))

    def gradient(c):
        normed = r.normed[c]
        g = (r.gs_own[c].astype(F32) + r.gs_in[c].astype(F32)) * r.gain_row[...]
        first_mean = jnp.mean(g, axis=1, keepdims=True)
        second_mean = jnp.mean(g * normed, axis=1, keepdims=True)
        own = r.grads[pl.ds(c * ndp, ndp)].astype(F32)
        return (own + r.inv_std[c] * (g - first_mean - normed * second_mean)).astype(BF16)

    back = [routed("b" + str(i), i < 2) for i in range(4)]

    def give(c):
        sums[2 * c].wait_recv()
        sums[2 * c + 1].wait_recv()
        rows = gradient(c)
        back[2 * c].start(rows[:, halves[0]])
        back[2 * c + 1].start(rows[:, halves[1]])

    give(0)
    ring1("a1", 0).wait_recv()
    send(ring2("a2", 0), r.a2_out, 0, cores(up, 0, 0) + r.a1_in[0].astype(F32))
    ring1("a1", 1).wait_recv()
    send(ring2("a2", 3), r.a2_out, 3, cores(down, 1, 0) + r.a1_in[1].astype(F32))

    def summed(i):
        r.bsum[i] = cores(order[i], xl, 1) + r.bx_in[i].astype(F32)

    x_first(0).wait_recv()
    summed(0)
    for s in range(2):
        send(ring1("b1", s), r.b1_out, s, r.bsum[0, s * part_rows : (s + 1) * part_rows])
    back[0].middle()
    x_first(1).wait_recv()
    summed(1)
    send(ring2("b2", 1), r.b2_out, 1, r.bsum[1, part_rows:])
    x_first(2).wait_recv()
    summed(2)
    send(ring2("b2", 2), r.b2_out, 2, r.bsum[2, :part_rows])
    give(1)
    mixes = [one_way("mx", c, partner) for c in range(2)]
    mix(2, r.mx_out, 0)
    mixes[0].start()
    back[1].middle()
    ring1("b1", 0).wait_recv()
    send(ring2("b2", 0), r.b2_out, 0, r.bsum[1, :part_rows] + r.b1_in[0].astype(F32))
    ring1("b1", 1).wait_recv()
    send(ring2("b2", 3), r.b2_out, 3, r.bsum[2, part_rows:] + r.b1_in[1].astype(F32))
    back[2].middle()
    mix(3, r.mx_out, 1)
    mixes[1].start()
    for slot in range(4):
        ring2("a2", slot).wait_recv()
    for s in range(2):
        r.total[s] = cores(y, s, 0) + r.a2_in[s].astype(F32) + r.a2_in[2 + s].astype(F32)
    r.ax_out[...] = r.total[1 - xl].astype(BF16)
    x_last = remote(r.ax_out, r.ax_in, r.ax_ss.at[0], r.ax_rs.at[0], x_device)
    x_last.start()
    back[3].middle()
    x_first(3).wait_recv()
    summed(3)
    for slot in range(4):
        ring2("b2", slot).wait_recv()
    over_z = [exchange("s" + str(b), nz, z, z_device) for b in range(2)]
    for s in range(2):
        at = slice(s * part_rows, (s + 1) * part_rows)
        r.bsum[3, at] = r.bsum[3, at] + r.b2_in[s].astype(F32) + r.b2_in[2 + s].astype(F32)
    r.s1_out[...] = r.bsum[3].astype(BF16).reshape(r.s1_out.shape)
    over_z[1].start()
    x_last.wait_recv()
    r.s0_out[...] = (r.total[xl] + r.ax_in[...].astype(F32)).astype(BF16).reshape(r.s0_out.shape)
    over_z[0].start()
    mix(1, r.mx_own, 1)

    r.rows[0, :, halves[0]] = back[0].finish()
    r.rows[0, :, halves[1]] = back[1].finish()
    for c in range(2):
        mixes[c].wait_recv()
    mixed_rows = []
    for c in range(2):
        slots = r.fr_out[c].astype(F32)
        frames = jnp.where(slots[:, :1] < 0.5 * ABSENT, slots, 0.0)
        mixed_rows.append((frames + 0.5 * (r.mx_own[c].astype(F32) + r.mx_in[c].astype(F32))).astype(BF16))
    r.mixed[...] = swap_rows(2, ndp, jnp.concatenate(mixed_rows, axis=0))
    for b in (1, 0):
        over_z[b].wait_recv()
        r.last_out[:, blocks[b]] = jnp.sum((r.s0_in, r.s1_in)[b][...].astype(F32), axis=0)
    last = remote(r.last_out, r.last_in, r.last_sem.at[0], r.last_sem.at[1], sibling)
    last.start()
    r.rows[1, :, halves[0]] = back[2].finish()
    r.rows[1, :, halves[1]] = back[3].finish()
    r.grad_source[...] = (t_dot(r.hot[:ndp], r.rows[0]) + t_dot(r.hot[ndp:], r.rows[1])).astype(BF16)

    last.wait_recv()
    own, other = r.last_out[...], r.last_in[...]
    count = own.shape[0] // 2
    is_low = core == 0
    own = jnp.where(is_low, own[:count], own[count:])
    other = jnp.where(is_low, other[:count], other[count:])
    r.grad_out[:, :half] = jnp.where(is_low, own, other)
    r.grad_out[:, half:] = jnp.where(is_low, other, own)

    last.wait_send()
    cot_copy.wait_send()
    x_last.wait_send()
    for copy in sums + mixes + frames_over + back + over_z:
        copy.wait_send()
    for name in ("a", "b"):
        for slot in range(2):
            ring1(name + "1", slot).wait_send()
        for slot in range(4):
            ring2(name + "2", slot).wait_send()
    for i in range(4):
        to_sibling(i).wait_send()
        x_first(i).wait_send()


def finish_kernel(mixed, grad_source, grad_out, mixed_out, grad_source_out, grad_out_out):
    mixed_out[...] = mixed[...]
    grad_source_out[...] = grad_source[...]
    grad_out_out[...] = grad_out[...]


def local(source_frames, routes, live_frames, norm_gain, weight_in, weight_out, cotangent):
    ndp = lax.axis_size("dp")
    nz = ndp // GROUP
    width, units = weight_in.shape
    half, strip = units // 2, width // ndp * 2
    block, tall = half // 2, width // 8
    vmem = pltpu.VMEM
    inputs = {
        "source": source_frames,
        "routes": routes.reshape(1, -1),
        "live": live_frames.reshape(1, 1),
        "gain": norm_gain,
        "cotangent": cotangent,
        "weight_in": weight_in,
        "weight_out": weight_out,
    }
    outputs = {
        "mixed": jax.ShapeDtypeStruct(cotangent.shape, BF16),
        "grad_source": jax.ShapeDtypeStruct(source_frames.shape, BF16),
        "grad_out": jax.ShapeDtypeStruct((width // ndp, units), F32),
    }
    scratch = {
        "win": vmem(weight_in.shape, BF16),
        "wout": vmem(weight_out.shape, BF16),
        "cot": vmem(cotangent.shape, BF16),
        "cot_in": vmem(cotangent.shape, BF16),
        "cot_sem": DMA((2,)),
        "cots": vmem((4 * ndp, width), BF16),
        "load_sem": DMA((3,)),
        "hot": vmem((2 * ndp, source_frames.shape[0]), BF16),
        "turned": vmem((width, 4 * ndp), BF16),
        "grads": vmem((4 * ndp, width), BF16),
        "act": vmem((4 * ndp, units), BF16),
        "gh": vmem((4 * ndp, units), BF16),
        "gain_row": vmem((1, width), F32),
        "scaled": vmem((ndp, width), BF16),
        "normed": vmem((2, ndp, width), F32),
        "inv_std": vmem((2, ndp, 1), F32),
        "gs_own": vmem((2, ndp, width), BF16),
        "mx_own": vmem((2, ndp, width), BF16),
        "rows": vmem((2, ndp, width), BF16),
        "mine": vmem((8, tall, half), F32),
        "total": vmem((2, tall, block), F32),
        "bsum": vmem((4, tall, block), F32),
        "last_out": vmem((strip, half), F32),
        "last_in": vmem((strip, half), F32),
        "last_sem": DMA((2,)),
    }

    def both_ways(name, shape, count):
        scratch[name + "_out"] = vmem(shape, BF16)
        scratch[name + "_in"] = vmem(shape, BF16)
        scratch[name + "_ss"] = DMA((count,))
        scratch[name + "_rs"] = DMA((count,))

    for prefix in "ab":
        for i in "0123":
            both_ways(prefix + i + "z", (nz, GROUP, width // 2), 1)
            both_ways(prefix + i + "j", (GROUP, nz, width // 2), 1)
    for name, count in (("fr", 4), ("gs", 4), ("mx", 2)):
        both_ways(name, (2, ndp, width), count)
    both_ways("sib", (8, tall, half), 4)
    both_ways("a1", (2, tall, block), 2)
    both_ways("a2", (4, tall, block), 4)
    both_ways("b1", (2, tall // 2, block), 2)
    both_ways("b2", (4, tall // 2, block), 4)
    both_ways("ax", (tall, block), 1)
    both_ways("bx", (4, tall, block), 4)
    both_ways("s0", (nz, strip, block), 1)
    both_ways("s1", (nz, strip, block), 1)

    in_vmem = pl.BlockSpec(memory_space=pltpu.VMEM)
    anywhere = pl.BlockSpec(memory_space=pl.ANY)
    from_hbm = ("weight_in", "weight_out", "cotangent")
    results = pl.pallas_call(
        functools.partial(kernel, ndp, list(inputs) + list(outputs) + list(scratch)),
        out_shape=list(outputs.values()),
        in_specs=[anywhere if name in from_hbm else in_vmem for name in inputs],
        out_specs=[in_vmem] * 3,
        scratch_shapes=list(scratch.values()),
        compiler_params=pltpu.CompilerParams(
            collective_id=1, has_side_effects=True, vmem_limit_bytes=60 * 1024 * 1024
        ),
        name="module",
    )(*inputs.values())
    mixed, grad_source, grad_out = pl.pallas_call(
        finish_kernel,
        out_shape=list(outputs.values()),
        in_specs=[in_vmem] * 3,
        out_specs=[in_vmem] * 3,
        name="finish",
    )(*results)
    return (mixed, grad_source, grad_out.T)


def solution(mesh):
    return jax.shard_map(
        local,
        mesh=mesh,
        in_specs=(
            P(("dp", "tensor"), None),
            P(("dp", "tensor"), None),
            P(("dp", "tensor")),
            P(),
            P(None, "tensor"),
            P("tensor", None),
            P(("dp", "tensor"), None),
        ),
        out_specs=(P(("dp", "tensor"), None), P(("dp", "tensor"), None), P("tensor", "dp")),
        check_vma=False,
    )
```

```python
import functools
from types import SimpleNamespace

import jax
import jax.numpy as jnp
from jax import lax
from jax.experimental import pallas as pl
from jax.experimental.pallas import tpu as pltpu
from jax.sharding import PartitionSpec as P

epsilon = 1e-05
ABSENT = 64.0
MESH = pl.DeviceIdType.MESH
GROUP = 16
RING = 4
DMA = pltpu.SemaphoreType.DMA
BF16, F32 = jnp.bfloat16, jnp.float32


def remote(src, dst, send_sem, recv_sem, device):
    return pltpu.make_async_remote_copy(
        src_ref=src, dst_ref=dst, send_sem=send_sem, recv_sem=recv_sem, device_id=device, device_id_type=MESH
    )


class Exchange:
    def __init__(self, n, place, device_of, buffers):
        self.n, self.place, self.device_of = n, place, device_of
        self.src, self.dst, self.send_sem, self.recv_sem = buffers

    def start(self):
        @pl.loop(1, self.n)
        def _(offset):
            p = (self.place + offset) & (self.n - 1)
            remote(
                self.src.at[p], self.dst.at[self.place], self.send_sem.at[0], self.recv_sem.at[0], self.device_of(p)
            ).start()

        self.dst[self.place] = self.src[self.place]

    def _all(self):
        part = pl.ds(0, self.n - 1)
        p = (self.place + 1) & (self.n - 1)
        return remote(self.src.at[part], self.dst.at[part], self.send_sem.at[0], self.recv_sem.at[0], self.device_of(p))

    def wait_recv(self):
        self._all().wait_recv()

    def wait_send(self):
        self._all().wait_send()


def picking(source, n):
    return (lax.broadcasted_iota(jnp.int32, (source.shape[0], n), 1) == source).astype(F32).astype(BF16)


def swap_rows(outer, inner, rows):
    n = outer * inner
    row = lax.broadcasted_iota(jnp.int32, (n, 1), 0)
    matrix = picking(lax.rem(row, outer) * inner + row // outer, n)
    return jnp.dot(matrix, rows, preferred_element_type=F32).astype(BF16)


def slot_matrix(routes_ref, live_ref, ndp, capacity):
    count = routes_ref.shape[1]
    row = lax.broadcasted_iota(jnp.int32, (count, count), 0)
    col = lax.broadcasted_iota(jnp.int32, (count, count), 1)
    target = routes_ref[...]
    wide = jnp.broadcast_to(target, (count, count))
    tall = jnp.sum(jnp.where(row == col, wide, 0), axis=1, keepdims=True)
    rank = jnp.sum(((tall == wide) & (row < col)).astype(jnp.int32), axis=0, keepdims=True)
    alive = lax.broadcasted_iota(jnp.int32, (1, count), 1) < live_ref[...]
    slot = jnp.where(alive, rank * ndp + target, -1)
    return (lax.broadcasted_iota(jnp.int32, (ndp * capacity, count), 0) == slot).astype(F32)


def dot_t(left, right):
    return lax.dot_general(left, right, (((1,), (1,)), ((), ())), preferred_element_type=F32)


def t_dot(left, right):
    return lax.dot_general(left, right, (((0,), (0,)), ((), ())), preferred_element_type=F32)


def tiles(total, size, body, start=0):
    @pl.loop(0, total // size)
    def _(i):
        body(pl.ds(pl.multiple_of(start + i * size, size), size))


class Route:
    def __init__(self, z_first, over_z, over_j):
        self.z_first = z_first
        self.nz, self.nj = over_z.n, over_j.n
        self.first, self.second = (over_z, over_j) if z_first else (over_j, over_z)

    def _send(self, exchange, rows):
        exchange.src[...] = rows.reshape(exchange.src.shape)
        exchange.start()

    def _got(self, exchange):
        exchange.wait_recv()
        shape = exchange.dst.shape
        return exchange.dst[...].reshape(shape[0] * shape[1], shape[2])

    def start(self, rows):
        self._send(self.first, rows if self.z_first else swap_rows(self.nz, self.nj, rows))

    def middle(self):
        a, b = (self.nz, self.nj) if self.z_first else (self.nj, self.nz)
        self._send(self.second, swap_rows(a, b, self._got(self.first)))

    def finish(self):
        rows = self._got(self.second)
        return swap_rows(self.nj, self.nz, rows) if self.z_first else rows

    def wait_send(self):
        self.first.wait_send()
        self.second.wait_send()


def kernel(ndp, names, *refs):
    r = SimpleNamespace(**dict(zip(names, refs)))
    me, t = lax.axis_index("dp"), lax.axis_index("tensor")
    nz = ndp // GROUP
    z, j = me // GROUP, lax.rem(me, GROUP)
    y, xl, core = j // 4, lax.rem(j // 2, 2), lax.rem(j, 2)
    z_device = lambda p: {"dp": p * GROUP + j}
    j_device = lambda p: {"dp": z * GROUP + p}
    y_device = lambda p: {"dp": z * GROUP + p * 4 + xl * 2 + core}
    x_device = {"dp": me + 2 - 4 * xl}
    sibling = {"dp": me + 1 - 2 * core}
    partner = {"dp": me + 2 - 4 * xl, "tensor": 1 - t}
    width = r.source.shape[1]
    units = r.win.shape[1]
    half = units // 2
    wide = width // 2
    halves = [slice(0, wide), slice(wide, width)]

    load_cot = pltpu.make_async_copy(r.cotangent, r.cot, r.load_sem.at[2])
    load_in = pltpu.make_async_copy(r.weight_in, r.win, r.load_sem.at[0])
    load_out = pltpu.make_async_copy(r.weight_out, r.wout, r.load_sem.at[1])
    load_cot.start()
    load_in.start()
    load_out.start()

    barrier = pltpu.get_barrier_semaphore()

    @pl.loop(1, nz)
    def _(offset):
        pl.semaphore_signal(barrier, inc=1, device_id=z_device(lax.rem(z + offset, nz)), device_id_type=MESH)

    @pl.loop(1, GROUP)
    def _(offset):
        pl.semaphore_signal(barrier, inc=1, device_id=j_device(lax.rem(j + offset, GROUP)), device_id_type=MESH)

    pl.semaphore_signal(barrier, inc=1, device_id=partner, device_id_type=MESH)

    def exchange(name, n, place, device_of):
        return Exchange(n, place, device_of, tuple(getattr(r, name + end) for end in ("_out", "_in", "_ss", "_rs")))

    def routed(name, z_first):
        return Route(z_first, exchange(name + "z", nz, z, z_device), exchange(name + "j", GROUP, j, j_device))

    def one_way(name, slot, device, part=None):
        out, land, ss, rs = (getattr(r, name + end) for end in ("_out", "_in", "_ss", "_rs"))
        index, sem = (slot, slot) if part is None else ((slot, slice(None), halves[part]), 2 * slot + part)
        return remote(out.at[index], land.at[index], ss.at[sem], rs.at[sem], device)

    r.gain_row[...] = r.gain[...].reshape(1, -1)
    hot = slot_matrix(r.routes, r.live, ndp, 2)
    r.hot[...] = hot.astype(BF16)
    first = lax.broadcasted_iota(jnp.int32, (ndp, width), 1) == 0

    def outgoing(rank):
        part = hot[rank * ndp : (rank + 1) * ndp]
        empty = jnp.sum(part, axis=1, keepdims=True) < 0.5
        rows = jnp.dot(part.astype(BF16), r.source[...], preferred_element_type=F32)
        return jnp.where(empty & first, ABSENT, rows).astype(BF16)

    there = [routed("a" + str(i), i < 2) for i in range(4)]
    leaving = outgoing(0)
    pl.semaphore_wait(barrier, nz + GROUP - 1)
    there[0].start(leaving[:, halves[0]])
    there[1].start(leaving[:, halves[1]])
    load_cot.wait()
    cot_copy = remote(r.cot, r.cot_in, r.cot_sem.at[0], r.cot_sem.at[1], partner)
    cot_copy.start()
    leaving = outgoing(1)
    there[2].start(leaving[:, halves[0]])
    there[3].start(leaving[:, halves[1]])

    strip = width // (nz * 8)
    step = width // RING

    def turn(side, rows):
        @pl.loop(0, RING)
        def _(i):
            row = lax.broadcasted_iota(jnp.int32, (step, 1), 0)
            x_at, z_at, rest = row // (step // 2), lax.rem(row // strip, nz), lax.rem(row, strip)
            pick = picking((z_at * 8 + i * 2 + x_at) * strip + rest, width)
            at = pl.ds(pl.multiple_of(i * step, step), step)
            r.turned[at, side * 2 * ndp : (side + 1) * 2 * ndp] = dot_t(pick, rows).astype(BF16)

    def order_cot(side, rows):
        rows = swap_rows(ndp, 2, rows)
        r.cots[side * 2 * ndp : (side + 1) * 2 * ndp] = rows
        turn(side, rows)

    order_cot(0, r.cot[...])
    there[0].middle()
    there[2].middle()
    load_in.wait()
    load_out.wait()

    def process(k):
        c = k % 2
        rows = pl.ds(k * ndp, ndp)
        slots = (r.fr_out if k < 2 else r.fr_in)[c].astype(F32)
        present = slots[:, :1] < 0.5 * ABSENT
        frames = jnp.where(present, slots, 0.0)
        centred = frames - jnp.mean(frames, axis=1, keepdims=True)
        inv_std = lax.rsqrt(jnp.mean(centred * centred, axis=1, keepdims=True) + epsilon)
        normed = centred * inv_std
        if k < 2:
            r.normed[c] = normed
            r.inv_std[c] = inv_std
        r.scaled[...] = (normed * r.gain_row[...]).astype(BF16)
        r.grads[rows] = jnp.where(present, r.cots[rows].astype(F32), 0.0).astype(BF16)

        def tile(n):
            hidden = jnp.dot(r.scaled[...], r.win[:, n], preferred_element_type=F32)
            grad_act = 0.5 * dot_t(r.grads[rows], r.wout[n, :])
            gate = jax.nn.sigmoid(hidden)
            r.act[rows, n] = jnp.where(present, hidden * gate, 0.0).astype(BF16)
            r.gh[rows, n] = (grad_act * gate * (1.0 + hidden * (1.0 - gate))).astype(BF16)

        tiles(units, 512, tile)

    def scaled_grad(k, out, c, start=0, length=None):
        def tile(n):
            out[c, :, n] = dot_t(r.gh[pl.ds(k * ndp, ndp), :], r.win[n, :]).astype(BF16)

        tiles(length or width, 384, tile, start)

    def mix(k, out, c):
        def tile(n):
            out[c, :, n] = jnp.dot(
                r.act[pl.ds(k * ndp, ndp), :], r.wout[:, n], preferred_element_type=F32
            ).astype(BF16)

        tiles(width, 512, tile)

    frames_over = [one_way("fr", i // 2, partner, i % 2) for i in range(4)]

    def land(i):
        r.fr_out[i // 2, :, halves[i % 2]] = there[i].finish()
        frames_over[i].start()

    there[1].middle()
    there[3].middle()
    land(0)
    land(1)
    process(0)
    scaled_grad(0, r.gs_own, 0)
    cot_copy.wait_recv()
    order_cot(1, r.cot_in[...])
    land(2)
    land(3)
    mix(0, r.mx_own, 0)
    frames_over[0].wait_recv()
    frames_over[1].wait_recv()
    process(2)
    sums = [one_way("gs", i // 2, partner, i % 2) for i in range(4)]

    def send_sums(c):
        for part in range(2):
            scaled_grad(2 + c, r.gs_out, c, part * wide, wide)
            sums[2 * c + part].start()

    send_sums(0)
    process(1)
    scaled_grad(1, r.gs_own, 1)
    for route in there:
        route.wait_send()
    frames_over[2].wait_recv()
    frames_over[3].wait_recv()
    process(3)
    send_sums(1)

    up, down, opposite = lax.rem(y + 1, RING), lax.rem(y + 3, RING), lax.rem(y + 2, RING)
    order = [opposite, up, down, y]

    def product(y_at, which):
        columns = pl.ds(pl.multiple_of(which * half, half), half)
        left = r.turned[pl.ds(pl.multiple_of(y_at * step, step), step), :]
        return (0.5 * jnp.dot(left, r.act[:, columns], preferred_element_type=F32)).reshape(2, step // 2, half)

    def to_sibling(i):
        part = pl.ds(2 * order[i], 2)
        return remote(r.sib_out.at[part], r.sib_in.at[part], r.sib_ss.at[i], r.sib_rs.at[i], sibling)

    for i in range(4):
        r.sib_out[pl.ds(2 * order[i], 2)] = product(order[i], 1 - core).astype(BF16)
        to_sibling(i).start()

    def keep(i):
        r.mine[pl.ds(2 * order[i], 2)] = product(order[i], core)
        to_sibling(i).wait_recv()

    block = half // 2
    blocks = [slice(0, block), slice(block, half)]
    part_rows = step // 4

    def cores(y_at, x_at, b):
        p = y_at * 2 + x_at
        return r.mine[p, :, blocks[b]] + r.sib_in[p, :, blocks[b]].astype(F32)

    def ring1(name, slot):
        return one_way(name, slot, y_device(down) if slot else y_device(up))

    def ring2(name, slot):
        return one_way(name, slot, y_device(down) if slot // 2 else y_device(up))

    def send(copy, buffer, index, value):
        buffer[index] = value.astype(BF16)
        copy.start()

    def x_first(i):
        return remote(r.bx_out.at[i], r.bx_in.at[i], r.bx_ss.at[i], r.bx_rs.at[i], x_device)

    keep(0)
    send(x_first(0), r.bx_out, 0, cores(opposite, 1 - xl, 1))
    for s in range(2):
        send(ring1("a1", s), r.a1_out, s, cores(opposite, s, 0))
    keep(1)
    send(x_first(1), r.bx_out, 1, cores(up, 1 - xl, 1))
    send(ring2("a2", 1), r.a2_out, 1, cores(up, 1, 0))
    keep(2)
    send(x_first(2), r.bx_out, 2, cores(down, 1 - xl, 1))
    send(ring2("a2", 2), r.a2_out, 2, cores(down, 0, 0))
    keep(3)
    send(x_first(3), r.bx_out, 3, cores(y, 1 - xl, 1))

    def gradient(c):
        normed = r.normed[c]
        g = (r.gs_own[c].astype(F32) + r.gs_in[c].astype(F32)) * r.gain_row[...]
        first_mean = jnp.mean(g, axis=1, keepdims=True)
        second_mean = jnp.mean(g * normed, axis=1, keepdims=True)
        own = r.grads[pl.ds(c * ndp, ndp)].astype(F32)
        return (own + r.inv_std[c] * (g - first_mean - normed * second_mean)).astype(BF16)

    back = [routed("b" + str(i), i < 2) for i in range(4)]

    def give(c):
        sums[2 * c].wait_recv()
        sums[2 * c + 1].wait_recv()
        rows = gradient(c)
        back[2 * c].start(rows[:, halves[0]])
        back[2 * c + 1].start(rows[:, halves[1]])

    give(0)
    ring1("a1", 0).wait_recv()
    send(ring2("a2", 0), r.a2_out, 0, cores(up, 0, 0) + r.a1_in[0].astype(F32))
    ring1("a1", 1).wait_recv()
    send(ring2("a2", 3), r.a2_out, 3, cores(down, 1, 0) + r.a1_in[1].astype(F32))

    def summed(i):
        r.bsum[i] = cores(order[i], xl, 1) + r.bx_in[i].astype(F32)

    x_first(0).wait_recv()
    summed(0)
    for s in range(2):
        send(ring1("b1", s), r.b1_out, s, r.bsum[0, s * part_rows : (s + 1) * part_rows])
    x_first(1).wait_recv()
    summed(1)
    send(ring2("b2", 1), r.b2_out, 1, r.bsum[1, part_rows:])
    give(1)
    x_first(2).wait_recv()
    summed(2)
    send(ring2("b2", 2), r.b2_out, 2, r.bsum[2, :part_rows])
    mixes = [one_way("mx", c, partner) for c in range(2)]
    mix(2, r.mx_out, 0)
    mixes[0].start()
    ring1("b1", 0).wait_recv()
    send(ring2("b2", 0), r.b2_out, 0, r.bsum[1, :part_rows] + r.b1_in[0].astype(F32))
    ring1("b1", 1).wait_recv()
    send(ring2("b2", 3), r.b2_out, 3, r.bsum[2, part_rows:] + r.b1_in[1].astype(F32))
    for slot in range(4):
        ring2("a2", slot).wait_recv()
    for s in range(2):
        r.total[s] = cores(y, s, 0) + r.a2_in[s].astype(F32) + r.a2_in[2 + s].astype(F32)
    r.ax_out[...] = r.total[1 - xl].astype(BF16)
    x_last = remote(r.ax_out, r.ax_in, r.ax_ss.at[0], r.ax_rs.at[0], x_device)
    x_last.start()
    back[2].middle()
    back[3].middle()
    mix(3, r.mx_out, 1)
    mixes[1].start()
    x_first(3).wait_recv()
    summed(3)
    for slot in range(4):
        ring2("b2", slot).wait_recv()
    over_z = [exchange("s" + str(b), nz, z, z_device) for b in range(2)]
    for s in range(2):
        at = slice(s * part_rows, (s + 1) * part_rows)
        r.bsum[3, at] = r.bsum[3, at] + r.b2_in[s].astype(F32) + r.b2_in[2 + s].astype(F32)
    r.s1_out[...] = r.bsum[3].astype(BF16).reshape(r.s1_out.shape)
    over_z[1].start()
    x_last.wait_recv()
    r.s0_out[...] = (r.total[xl] + r.ax_in[...].astype(F32)).astype(BF16).reshape(r.s0_out.shape)
    over_z[0].start()
    back[0].middle()
    back[1].middle()
    mix(1, r.mx_own, 1)

    r.rows[0, :, halves[0]] = back[0].finish()
    r.rows[0, :, halves[1]] = back[1].finish()
    for b in (1, 0):
        over_z[b].wait_recv()
        r.last_out[:, blocks[b]] = jnp.sum((r.s0_in, r.s1_in)[b][...].astype(F32), axis=0)
    last = remote(r.last_out, r.last_in, r.last_sem.at[0], r.last_sem.at[1], sibling)
    last.start()
    for c in range(2):
        mixes[c].wait_recv()
    mixed_rows = []
    for c in range(2):
        slots = r.fr_out[c].astype(F32)
        frames = jnp.where(slots[:, :1] < 0.5 * ABSENT, slots, 0.0)
        mixed_rows.append((frames + 0.5 * (r.mx_own[c].astype(F32) + r.mx_in[c].astype(F32))).astype(BF16))
    r.mixed[...] = swap_rows(2, ndp, jnp.concatenate(mixed_rows, axis=0))
    r.rows[1, :, halves[0]] = back[2].finish()
    r.rows[1, :, halves[1]] = back[3].finish()
    r.grad_source[...] = (t_dot(r.hot[:ndp], r.rows[0]) + t_dot(r.hot[ndp:], r.rows[1])).astype(BF16)

    last.wait_recv()
    own, other = r.last_out[...], r.last_in[...]
    count = own.shape[0] // 2
    is_low = core == 0
    own = jnp.where(is_low, own[:count], own[count:])
    other = jnp.where(is_low, other[:count], other[count:])
    r.grad_out[:, :half] = jnp.where(is_low, own, other)
    r.grad_out[:, half:] = jnp.where(is_low, other, own)

    last.wait_send()
    cot_copy.wait_send()
    x_last.wait_send()
    for copy in sums + mixes + frames_over + back + over_z:
        copy.wait_send()
    for name in ("a", "b"):
        for slot in range(2):
            ring1(name + "1", slot).wait_send()
        for slot in range(4):
            ring2(name + "2", slot).wait_send()
    for i in range(4):
        to_sibling(i).wait_send()
        x_first(i).wait_send()


def finish_kernel(mixed, grad_source, grad_out, mixed_out, grad_source_out, grad_out_out):
    mixed_out[...] = mixed[...]
    grad_source_out[...] = grad_source[...]
    grad_out_out[...] = grad_out[...]


def local(source_frames, routes, live_frames, norm_gain, weight_in, weight_out, cotangent):
    ndp = lax.axis_size("dp")
    nz = ndp // GROUP
    width, units = weight_in.shape
    half, strip = units // 2, width // ndp * 2
    block, tall = half // 2, width // 8
    vmem = pltpu.VMEM
    inputs = {
        "source": source_frames,
        "routes": routes.reshape(1, -1),
        "live": live_frames.reshape(1, 1),
        "gain": norm_gain,
        "cotangent": cotangent,
        "weight_in": weight_in,
        "weight_out": weight_out,
    }
    outputs = {
        "mixed": jax.ShapeDtypeStruct(cotangent.shape, BF16),
        "grad_source": jax.ShapeDtypeStruct(source_frames.shape, BF16),
        "grad_out": jax.ShapeDtypeStruct((width // ndp, units), F32),
    }
    scratch = {
        "win": vmem(weight_in.shape, BF16),
        "wout": vmem(weight_out.shape, BF16),
        "cot": vmem(cotangent.shape, BF16),
        "cot_in": vmem(cotangent.shape, BF16),
        "cot_sem": DMA((2,)),
        "cots": vmem((4 * ndp, width), BF16),
        "load_sem": DMA((3,)),
        "hot": vmem((2 * ndp, source_frames.shape[0]), BF16),
        "turned": vmem((width, 4 * ndp), BF16),
        "grads": vmem((4 * ndp, width), BF16),
        "act": vmem((4 * ndp, units), BF16),
        "gh": vmem((4 * ndp, units), BF16),
        "gain_row": vmem((1, width), F32),
        "scaled": vmem((ndp, width), BF16),
        "normed": vmem((2, ndp, width), F32),
        "inv_std": vmem((2, ndp, 1), F32),
        "gs_own": vmem((2, ndp, width), BF16),
        "mx_own": vmem((2, ndp, width), BF16),
        "rows": vmem((2, ndp, width), BF16),
        "mine": vmem((8, tall, half), F32),
        "total": vmem((2, tall, block), F32),
        "bsum": vmem((4, tall, block), F32),
        "last_out": vmem((strip, half), F32),
        "last_in": vmem((strip, half), F32),
        "last_sem": DMA((2,)),
    }

    def both_ways(name, shape, count):
        scratch[name + "_out"] = vmem(shape, BF16)
        scratch[name + "_in"] = vmem(shape, BF16)
        scratch[name + "_ss"] = DMA((count,))
        scratch[name + "_rs"] = DMA((count,))

    for prefix in "ab":
        for i in "0123":
            both_ways(prefix + i + "z", (nz, GROUP, width // 2), 1)
            both_ways(prefix + i + "j", (GROUP, nz, width // 2), 1)
    for name, count in (("fr", 4), ("gs", 4), ("mx", 2)):
        both_ways(name, (2, ndp, width), count)
    both_ways("sib", (8, tall, half), 4)
    both_ways("a1", (2, tall, block), 2)
    both_ways("a2", (4, tall, block), 4)
    both_ways("b1", (2, tall // 2, block), 2)
    both_ways("b2", (4, tall // 2, block), 4)
    both_ways("ax", (tall, block), 1)
    both_ways("bx", (4, tall, block), 4)
    both_ways("s0", (nz, strip, block), 1)
    both_ways("s1", (nz, strip, block), 1)

    in_vmem = pl.BlockSpec(memory_space=pltpu.VMEM)
    anywhere = pl.BlockSpec(memory_space=pl.ANY)
    from_hbm = ("weight_in", "weight_out", "cotangent")
    results = pl.pallas_call(
        functools.partial(kernel, ndp, list(inputs) + list(outputs) + list(scratch)),
        out_shape=list(outputs.values()),
        in_specs=[anywhere if name in from_hbm else in_vmem for name in inputs],
        out_specs=[in_vmem] * 3,
        scratch_shapes=list(scratch.values()),
        compiler_params=pltpu.CompilerParams(
            collective_id=1, has_side_effects=True, vmem_limit_bytes=60 * 1024 * 1024
        ),
        name="module",
    )(*inputs.values())
    mixed, grad_source, grad_out = pl.pallas_call(
        finish_kernel,
        out_shape=list(outputs.values()),
        in_specs=[in_vmem] * 3,
        out_specs=[in_vmem] * 3,
        name="finish",
    )(*results)
    return (mixed, grad_source, grad_out.T)


def solution(mesh):
    return jax.shard_map(
        local,
        mesh=mesh,
        in_specs=(
            P(("dp", "tensor"), None),
            P(("dp", "tensor"), None),
            P(("dp", "tensor")),
            P(),
            P(None, "tensor"),
            P("tensor", None),
            P(("dp", "tensor"), None),
        ),
        out_specs=(P(("dp", "tensor"), None), P(("dp", "tensor"), None), P("tensor", "dp")),
        check_vma=False,
    )
```

```python
import functools
from types import SimpleNamespace

import jax
import jax.numpy as jnp
from jax import lax
from jax.experimental import pallas as pl
from jax.experimental.pallas import tpu as pltpu
from jax.sharding import PartitionSpec as P

epsilon = 1e-05
ABSENT = 64.0
MESH = pl.DeviceIdType.MESH
GROUP = 16
RING = 4
DMA = pltpu.SemaphoreType.DMA
BF16, F32 = jnp.bfloat16, jnp.float32


def remote(src, dst, send_sem, recv_sem, device):
    return pltpu.make_async_remote_copy(
        src_ref=src, dst_ref=dst, send_sem=send_sem, recv_sem=recv_sem, device_id=device, device_id_type=MESH
    )


class Exchange:
    def __init__(self, n, place, device_of, buffers):
        self.n, self.place, self.device_of = n, place, device_of
        self.src, self.dst, self.send_sem, self.recv_sem = buffers

    def start(self):
        @pl.loop(1, self.n)
        def _(offset):
            p = (self.place + offset) & (self.n - 1)
            remote(
                self.src.at[p], self.dst.at[self.place], self.send_sem.at[0], self.recv_sem.at[0], self.device_of(p)
            ).start()

        self.dst[self.place] = self.src[self.place]

    def _all(self):
        part = pl.ds(0, self.n - 1)
        p = (self.place + 1) & (self.n - 1)
        return remote(self.src.at[part], self.dst.at[part], self.send_sem.at[0], self.recv_sem.at[0], self.device_of(p))

    def wait_recv(self):
        self._all().wait_recv()

    def wait_send(self):
        self._all().wait_send()


def picking(source, n):
    return (lax.broadcasted_iota(jnp.int32, (source.shape[0], n), 1) == source).astype(F32).astype(BF16)


def swap_rows(outer, inner, rows):
    n = outer * inner
    row = lax.broadcasted_iota(jnp.int32, (n, 1), 0)
    matrix = picking(lax.rem(row, outer) * inner + row // outer, n)
    return jnp.dot(matrix, rows, preferred_element_type=F32).astype(BF16)


def slot_matrix(routes_ref, live_ref, ndp, capacity):
    count = routes_ref.shape[1]
    row = lax.broadcasted_iota(jnp.int32, (count, count), 0)
    col = lax.broadcasted_iota(jnp.int32, (count, count), 1)
    target = routes_ref[...]
    wide = jnp.broadcast_to(target, (count, count))
    tall = jnp.sum(jnp.where(row == col, wide, 0), axis=1, keepdims=True)
    rank = jnp.sum(((tall == wide) & (row < col)).astype(jnp.int32), axis=0, keepdims=True)
    alive = lax.broadcasted_iota(jnp.int32, (1, count), 1) < live_ref[...]
    slot = jnp.where(alive, rank * ndp + target, -1)
    return (lax.broadcasted_iota(jnp.int32, (ndp * capacity, count), 0) == slot).astype(F32)


def dot_t(left, right):
    return lax.dot_general(left, right, (((1,), (1,)), ((), ())), preferred_element_type=F32)


def t_dot(left, right):
    return lax.dot_general(left, right, (((0,), (0,)), ((), ())), preferred_element_type=F32)


def tiles(total, size, body, start=0):
    @pl.loop(0, total // size)
    def _(i):
        body(pl.ds(pl.multiple_of(start + i * size, size), size))


class Route:
    def __init__(self, z_first, over_z, over_j):
        self.z_first = z_first
        self.nz, self.nj = over_z.n, over_j.n
        self.first, self.second = (over_z, over_j) if z_first else (over_j, over_z)

    def _send(self, exchange, rows):
        exchange.src[...] = rows.reshape(exchange.src.shape)
        exchange.start()

    def _got(self, exchange):
        exchange.wait_recv()
        shape = exchange.dst.shape
        return exchange.dst[...].reshape(shape[0] * shape[1], shape[2])

    def start(self, rows):
        self._send(self.first, rows if self.z_first else swap_rows(self.nz, self.nj, rows))

    def middle(self):
        a, b = (self.nz, self.nj) if self.z_first else (self.nj, self.nz)
        self._send(self.second, swap_rows(a, b, self._got(self.first)))

    def finish(self):
        rows = self._got(self.second)
        return swap_rows(self.nj, self.nz, rows) if self.z_first else rows

    def wait_send(self):
        self.first.wait_send()
        self.second.wait_send()


def kernel(ndp, names, *refs):
    r = SimpleNamespace(**dict(zip(names, refs)))
    me, t = lax.axis_index("dp"), lax.axis_index("tensor")
    nz = ndp // GROUP
    z, j = me // GROUP, lax.rem(me, GROUP)
    y, xl, core = j // 4, lax.rem(j // 2, 2), lax.rem(j, 2)
    z_device = lambda p: {"dp": p * GROUP + j}
    j_device = lambda p: {"dp": z * GROUP + p}
    y_device = lambda p: {"dp": z * GROUP + p * 4 + xl * 2 + core}
    x_device = {"dp": me + 2 - 4 * xl}
    sibling = {"dp": me + 1 - 2 * core}
    partner = {"dp": me + 2 - 4 * xl, "tensor": 1 - t}
    width = r.source.shape[1]
    units = r.win.shape[1]
    half = units // 2
    wide = width // 2
    halves = [slice(0, wide), slice(wide, width)]

    load_cot = pltpu.make_async_copy(r.cotangent, r.cot, r.load_sem.at[2])
    load_in = pltpu.make_async_copy(r.weight_in, r.win, r.load_sem.at[0])
    load_out = pltpu.make_async_copy(r.weight_out, r.wout, r.load_sem.at[1])
    load_cot.start()
    load_in.start()
    load_out.start()

    barrier = pltpu.get_barrier_semaphore()

    @pl.loop(1, nz)
    def _(offset):
        pl.semaphore_signal(barrier, inc=1, device_id=z_device(lax.rem(z + offset, nz)), device_id_type=MESH)

    @pl.loop(1, GROUP)
    def _(offset):
        pl.semaphore_signal(barrier, inc=1, device_id=j_device(lax.rem(j + offset, GROUP)), device_id_type=MESH)

    pl.semaphore_signal(barrier, inc=1, device_id=partner, device_id_type=MESH)

    def exchange(name, n, place, device_of):
        return Exchange(n, place, device_of, tuple(getattr(r, name + end) for end in ("_out", "_in", "_ss", "_rs")))

    def routed(name, z_first):
        return Route(z_first, exchange(name + "z", nz, z, z_device), exchange(name + "j", GROUP, j, j_device))

    def one_way(name, slot, device, part=None):
        out, land, ss, rs = (getattr(r, name + end) for end in ("_out", "_in", "_ss", "_rs"))
        index, sem = (slot, slot) if part is None else ((slot, slice(None), halves[part]), 2 * slot + part)
        return remote(out.at[index], land.at[index], ss.at[sem], rs.at[sem], device)

    r.gain_row[...] = r.gain[...].reshape(1, -1)
    hot = slot_matrix(r.routes, r.live, ndp, 2)
    r.hot[...] = hot.astype(BF16)
    first = lax.broadcasted_iota(jnp.int32, (ndp, width), 1) == 0

    def outgoing(rank):
        part = hot[rank * ndp : (rank + 1) * ndp]
        empty = jnp.sum(part, axis=1, keepdims=True) < 0.5
        rows = jnp.dot(part.astype(BF16), r.source[...], preferred_element_type=F32)
        return jnp.where(empty & first, ABSENT, rows).astype(BF16)

    there = [routed("a" + str(i), i < 2) for i in range(4)]
    leaving = outgoing(0)
    load_cot.wait()
    cot_copy = remote(r.cot, r.cot_in, r.cot_sem.at[0], r.cot_sem.at[1], partner)
    pl.semaphore_wait(barrier, nz + GROUP - 1)
    cot_copy.start()
    there[0].start(leaving[:, halves[0]])
    there[1].start(leaving[:, halves[1]])
    leaving = outgoing(1)
    there[2].start(leaving[:, halves[0]])
    there[3].start(leaving[:, halves[1]])

    strip = width // (nz * 8)
    step = width // RING

    def turn(side, rows):
        @pl.loop(0, RING)
        def _(i):
            row = lax.broadcasted_iota(jnp.int32, (step, 1), 0)
            x_at, z_at, rest = row // (step // 2), lax.rem(row // strip, nz), lax.rem(row, strip)
            pick = picking((z_at * 8 + i * 2 + x_at) * strip + rest, width)
            at = pl.ds(pl.multiple_of(i * step, step), step)
            r.turned[at, side * 2 * ndp : (side + 1) * 2 * ndp] = dot_t(pick, rows).astype(BF16)

    def order_cot(side, rows):
        rows = swap_rows(ndp, 2, rows)
        r.cots[side * 2 * ndp : (side + 1) * 2 * ndp] = rows
        turn(side, rows)

    order_cot(0, r.cot[...])
    there[0].middle()
    there[2].middle()
    load_in.wait()
    load_out.wait()

    def process(k):
        c = k % 2
        rows = pl.ds(k * ndp, ndp)
        slots = (r.fr_out if k < 2 else r.fr_in)[c].astype(F32)
        present = slots[:, :1] < 0.5 * ABSENT
        frames = jnp.where(present, slots, 0.0)
        centred = frames - jnp.mean(frames, axis=1, keepdims=True)
        inv_std = lax.rsqrt(jnp.mean(centred * centred, axis=1, keepdims=True) + epsilon)
        normed = centred * inv_std
        if k < 2:
            r.normed[c] = normed
            r.inv_std[c] = inv_std
        r.scaled[...] = (normed * r.gain_row[...]).astype(BF16)
        r.grads[rows] = jnp.where(present, r.cots[rows].astype(F32), 0.0).astype(BF16)

        def tile(n):
            hidden = jnp.dot(r.scaled[...], r.win[:, n], preferred_element_type=F32)
            grad_act = 0.5 * dot_t(r.grads[rows], r.wout[n, :])
            gate = jax.nn.sigmoid(hidden)
            r.act[rows, n] = jnp.where(present, hidden * gate, 0.0).astype(BF16)
            r.gh[rows, n] = (grad_act * gate * (1.0 + hidden * (1.0 - gate))).astype(BF16)

        tiles(units, 512, tile)

    def scaled_grad(k, out, c, start=0, length=None):
        def tile(n):
            out[c, :, n] = dot_t(r.gh[pl.ds(k * ndp, ndp), :], r.win[n, :]).astype(BF16)

        tiles(length or width, 384, tile, start)

    def mix(k, out, c):
        def tile(n):
            out[c, :, n] = jnp.dot(
                r.act[pl.ds(k * ndp, ndp), :], r.wout[:, n], preferred_element_type=F32
            ).astype(BF16)

        tiles(width, 512, tile)

    frames_over = [one_way("fr", i // 2, partner, i % 2) for i in range(4)]

    def land(i):
        r.fr_out[i // 2, :, halves[i % 2]] = there[i].finish()
        frames_over[i].start()

    there[1].middle()
    there[3].middle()
    land(0)
    land(1)
    process(0)
    scaled_grad(0, r.gs_own, 0)
    cot_copy.wait_recv()
    order_cot(1, r.cot_in[...])
    land(2)
    land(3)
    process(1)
    frames_over[0].wait_recv()
    frames_over[1].wait_recv()
    process(2)
    sums = [one_way("gs", i // 2, partner, i % 2) for i in range(4)]
    scaled_grad(2, r.gs_out, 0)
    scaled_grad(1, r.gs_own, 1)
    mix(0, r.mx_own, 0)
    frames_over[2].wait_recv()
    frames_over[3].wait_recv()
    sums[0].start()
    sums[1].start()
    process(3)
    for part in range(2):
        scaled_grad(3, r.gs_out, 1, part * wide, wide)
        sums[2 + part].start()

    up, down, opposite = lax.rem(y + 1, RING), lax.rem(y + 3, RING), lax.rem(y + 2, RING)
    order = [opposite, up, down, y]

    def product(y_at, which):
        columns = pl.ds(pl.multiple_of(which * half, half), half)
        left = r.turned[pl.ds(pl.multiple_of(y_at * step, step), step), :]
        return (0.5 * jnp.dot(left, r.act[:, columns], preferred_element_type=F32)).reshape(2, step // 2, half)

    def to_sibling(i):
        part = pl.ds(2 * order[i], 2)
        return remote(r.sib_out.at[part], r.sib_in.at[part], r.sib_ss.at[i], r.sib_rs.at[i], sibling)

    for i in range(4):
        r.sib_out[pl.ds(2 * order[i], 2)] = product(order[i], 1 - core).astype(BF16)
        to_sibling(i).start()

    def keep(i):
        r.mine[pl.ds(2 * order[i], 2)] = product(order[i], core)
        to_sibling(i).wait_recv()

    block = half // 2
    blocks = [slice(0, block), slice(block, half)]
    part_rows = step // 4

    def cores(y_at, x_at, b):
        p = y_at * 2 + x_at
        return r.mine[p, :, blocks[b]] + r.sib_in[p, :, blocks[b]].astype(F32)

    def ring1(name, slot):
        return one_way(name, slot, y_device(down) if slot else y_device(up))

    def ring2(name, slot):
        return one_way(name, slot, y_device(down) if slot // 2 else y_device(up))

    def send(copy, buffer, index, value):
        buffer[index] = value.astype(BF16)
        copy.start()

    def x_first(i):
        return remote(r.bx_out.at[i], r.bx_in.at[i], r.bx_ss.at[i], r.bx_rs.at[i], x_device)

    keep(0)
    send(x_first(0), r.bx_out, 0, cores(opposite, 1 - xl, 1))
    for s in range(2):
        send(ring1("a1", s), r.a1_out, s, cores(opposite, s, 0))
    keep(1)
    send(x_first(1), r.bx_out, 1, cores(up, 1 - xl, 1))
    send(ring2("a2", 1), r.a2_out, 1, cores(up, 1, 0))
    keep(2)
    send(x_first(2), r.bx_out, 2, cores(down, 1 - xl, 1))
    send(ring2("a2", 2), r.a2_out, 2, cores(down, 0, 0))
    keep(3)
    send(x_first(3), r.bx_out, 3, cores(y, 1 - xl, 1))

    def gradient(c):
        normed = r.normed[c]
        g = (r.gs_own[c].astype(F32) + r.gs_in[c].astype(F32)) * r.gain_row[...]
        first_mean = jnp.mean(g, axis=1, keepdims=True)
        second_mean = jnp.mean(g * normed, axis=1, keepdims=True)
        own = r.grads[pl.ds(c * ndp, ndp)].astype(F32)
        return (own + r.inv_std[c] * (g - first_mean - normed * second_mean)).astype(BF16)

    back = [routed("b" + str(i), i < 2) for i in range(4)]

    def give(c):
        sums[2 * c].wait_recv()
        sums[2 * c + 1].wait_recv()
        rows = gradient(c)
        back[2 * c].start(rows[:, halves[0]])
        back[2 * c + 1].start(rows[:, halves[1]])

    give(0)
    ring1("a1", 0).wait_recv()
    send(ring2("a2", 0), r.a2_out, 0, cores(up, 0, 0) + r.a1_in[0].astype(F32))
    ring1("a1", 1).wait_recv()
    send(ring2("a2", 3), r.a2_out, 3, cores(down, 1, 0) + r.a1_in[1].astype(F32))

    def summed(i):
        r.bsum[i] = cores(order[i], xl, 1) + r.bx_in[i].astype(F32)

    x_first(0).wait_recv()
    summed(0)
    for s in range(2):
        send(ring1("b1", s), r.b1_out, s, r.bsum[0, s * part_rows : (s + 1) * part_rows])
    x_first(1).wait_recv()
    summed(1)
    send(ring2("b2", 1), r.b2_out, 1, r.bsum[1, part_rows:])
    give(1)
    x_first(2).wait_recv()
    summed(2)
    send(ring2("b2", 2), r.b2_out, 2, r.bsum[2, :part_rows])
    mixes = [one_way("mx", c, partner) for c in range(2)]
    mix(2, r.mx_out, 0)
    mixes[0].start()
    ring1("b1", 0).wait_recv()
    send(ring2("b2", 0), r.b2_out, 0, r.bsum[1, :part_rows] + r.b1_in[0].astype(F32))
    ring1("b1", 1).wait_recv()
    send(ring2("b2", 3), r.b2_out, 3, r.bsum[2, part_rows:] + r.b1_in[1].astype(F32))
    for slot in range(4):
        ring2("a2", slot).wait_recv()
    for s in range(2):
        r.total[s] = cores(y, s, 0) + r.a2_in[s].astype(F32) + r.a2_in[2 + s].astype(F32)
    r.ax_out[...] = r.total[1 - xl].astype(BF16)
    x_last = remote(r.ax_out, r.ax_in, r.ax_ss.at[0], r.ax_rs.at[0], x_device)
    x_last.start()
    back[2].middle()
    back[3].middle()
    mix(3, r.mx_out, 1)
    mixes[1].start()
    x_first(3).wait_recv()
    summed(3)
    for slot in range(4):
        ring2("b2", slot).wait_recv()
    over_z = [exchange("s" + str(b), nz, z, z_device) for b in range(2)]
    for s in range(2):
        at = slice(s * part_rows, (s + 1) * part_rows)
        r.bsum[3, at] = r.bsum[3, at] + r.b2_in[s].astype(F32) + r.b2_in[2 + s].astype(F32)
    r.s1_out[...] = r.bsum[3].astype(BF16).reshape(r.s1_out.shape)
    over_z[1].start()
    x_last.wait_recv()
    r.s0_out[...] = (r.total[xl] + r.ax_in[...].astype(F32)).astype(BF16).reshape(r.s0_out.shape)
    over_z[0].start()
    back[0].middle()
    back[1].middle()
    mix(1, r.mx_own, 1)
    x_last.wait_send()
    cot_copy.wait_send()
    for copy in sums + frames_over + there:
        copy.wait_send()
    for name in ("a", "b"):
        for slot in range(2):
            ring1(name + "1", slot).wait_send()
        for slot in range(4):
            ring2(name + "2", slot).wait_send()
    for i in range(4):
        to_sibling(i).wait_send()
        x_first(i).wait_send()

    r.rows[0, :, halves[0]] = back[0].finish()
    r.rows[0, :, halves[1]] = back[1].finish()
    for b in (1, 0):
        over_z[b].wait_recv()
        r.last_out[:, blocks[b]] = jnp.sum((r.s0_in, r.s1_in)[b][...].astype(F32), axis=0)
    last = remote(r.last_out, r.last_in, r.last_sem.at[0], r.last_sem.at[1], sibling)
    last.start()
    for c in range(2):
        mixes[c].wait_recv()
    mixed_rows = []
    for c in range(2):
        slots = r.fr_out[c].astype(F32)
        frames = jnp.where(slots[:, :1] < 0.5 * ABSENT, slots, 0.0)
        mixed_rows.append((frames + 0.5 * (r.mx_own[c].astype(F32) + r.mx_in[c].astype(F32))).astype(BF16))
    r.mixed[...] = swap_rows(2, ndp, jnp.concatenate(mixed_rows, axis=0))
    r.rows[1, :, halves[0]] = back[2].finish()
    r.rows[1, :, halves[1]] = back[3].finish()
    r.grad_source[...] = (t_dot(r.hot[:ndp], r.rows[0]) + t_dot(r.hot[ndp:], r.rows[1])).astype(BF16)

    last.wait_recv()
    own, other = r.last_out[...], r.last_in[...]
    count = own.shape[0] // 2
    is_low = core == 0
    own = jnp.where(is_low, own[:count], own[count:])
    other = jnp.where(is_low, other[:count], other[count:])
    r.grad_out[:, :half] = jnp.where(is_low, own, other)
    r.grad_out[:, half:] = jnp.where(is_low, other, own)

    last.wait_send()
    for copy in mixes + back + over_z:
        copy.wait_send()


def finish_kernel(mixed, grad_source, grad_out, mixed_out, grad_source_out, grad_out_out):
    mixed_out[...] = mixed[...]
    grad_source_out[...] = grad_source[...]
    grad_out_out[...] = grad_out[...]


def local(source_frames, routes, live_frames, norm_gain, weight_in, weight_out, cotangent):
    ndp = lax.axis_size("dp")
    nz = ndp // GROUP
    width, units = weight_in.shape
    half, strip = units // 2, width // ndp * 2
    block, tall = half // 2, width // 8
    vmem = pltpu.VMEM
    inputs = {
        "source": source_frames,
        "routes": routes.reshape(1, -1),
        "live": live_frames.reshape(1, 1),
        "gain": norm_gain,
        "cotangent": cotangent,
        "weight_in": weight_in,
        "weight_out": weight_out,
    }
    outputs = {
        "mixed": jax.ShapeDtypeStruct(cotangent.shape, BF16),
        "grad_source": jax.ShapeDtypeStruct(source_frames.shape, BF16),
        "grad_out": jax.ShapeDtypeStruct((width // ndp, units), F32),
    }
    scratch = {
        "win": vmem(weight_in.shape, BF16),
        "wout": vmem(weight_out.shape, BF16),
        "cot": vmem(cotangent.shape, BF16),
        "cot_in": vmem(cotangent.shape, BF16),
        "cot_sem": DMA((2,)),
        "cots": vmem((4 * ndp, width), BF16),
        "load_sem": DMA((3,)),
        "hot": vmem((2 * ndp, source_frames.shape[0]), BF16),
        "turned": vmem((width, 4 * ndp), BF16),
        "grads": vmem((4 * ndp, width), BF16),
        "act": vmem((4 * ndp, units), BF16),
        "gh": vmem((4 * ndp, units), BF16),
        "gain_row": vmem((1, width), F32),
        "scaled": vmem((ndp, width), BF16),
        "normed": vmem((2, ndp, width), F32),
        "inv_std": vmem((2, ndp, 1), F32),
        "gs_own": vmem((2, ndp, width), BF16),
        "mx_own": vmem((2, ndp, width), BF16),
        "rows": vmem((2, ndp, width), BF16),
        "mine": vmem((8, tall, half), F32),
        "total": vmem((2, tall, block), F32),
        "bsum": vmem((4, tall, block), F32),
        "last_out": vmem((strip, half), F32),
        "last_in": vmem((strip, half), F32),
        "last_sem": DMA((2,)),
    }

    def both_ways(name, shape, count):
        scratch[name + "_out"] = vmem(shape, BF16)
        scratch[name + "_in"] = vmem(shape, BF16)
        scratch[name + "_ss"] = DMA((count,))
        scratch[name + "_rs"] = DMA((count,))

    for prefix in "ab":
        for i in "0123":
            both_ways(prefix + i + "z", (nz, GROUP, width // 2), 1)
            both_ways(prefix + i + "j", (GROUP, nz, width // 2), 1)
    for name, count in (("fr", 4), ("gs", 4), ("mx", 2)):
        both_ways(name, (2, ndp, width), count)
    both_ways("sib", (8, tall, half), 4)
    both_ways("a1", (2, tall, block), 2)
    both_ways("a2", (4, tall, block), 4)
    both_ways("b1", (2, tall // 2, block), 2)
    both_ways("b2", (4, tall // 2, block), 4)
    both_ways("ax", (tall, block), 1)
    both_ways("bx", (4, tall, block), 4)
    both_ways("s0", (nz, strip, block), 1)
    both_ways("s1", (nz, strip, block), 1)

    in_vmem = pl.BlockSpec(memory_space=pltpu.VMEM)
    anywhere = pl.BlockSpec(memory_space=pl.ANY)
    from_hbm = ("weight_in", "weight_out", "cotangent")
    results = pl.pallas_call(
        functools.partial(kernel, ndp, list(inputs) + list(outputs) + list(scratch)),
        out_shape=list(outputs.values()),
        in_specs=[anywhere if name in from_hbm else in_vmem for name in inputs],
        out_specs=[in_vmem] * 3,
        scratch_shapes=list(scratch.values()),
        compiler_params=pltpu.CompilerParams(
            collective_id=1, has_side_effects=True, vmem_limit_bytes=60 * 1024 * 1024
        ),
        name="module",
    )(*inputs.values())
    mixed, grad_source, grad_out = pl.pallas_call(
        finish_kernel,
        out_shape=list(outputs.values()),
        in_specs=[in_vmem] * 3,
        out_specs=[in_vmem] * 3,
        name="finish",
    )(*results)
    return (mixed, grad_source, grad_out.T)


def solution(mesh):
    return jax.shard_map(
        local,
        mesh=mesh,
        in_specs=(
            P(("dp", "tensor"), None),
            P(("dp", "tensor"), None),
            P(("dp", "tensor")),
            P(),
            P(None, "tensor"),
            P("tensor", None),
            P(("dp", "tensor"), None),
        ),
        out_specs=(P(("dp", "tensor"), None), P(("dp", "tensor"), None), P("tensor", "dp")),
        check_vma=False,
    )
```

```python
import functools
from types import SimpleNamespace

import jax
import jax.numpy as jnp
from jax import lax
from jax.experimental import pallas as pl
from jax.experimental.pallas import tpu as pltpu
from jax.sharding import PartitionSpec as P

epsilon = 1e-05
ABSENT = 64.0
MESH = pl.DeviceIdType.MESH
GROUP = 16
RING = 4
DMA = pltpu.SemaphoreType.DMA
BF16, F32 = jnp.bfloat16, jnp.float32


def remote(src, dst, send_sem, recv_sem, device):
    return pltpu.make_async_remote_copy(
        src_ref=src, dst_ref=dst, send_sem=send_sem, recv_sem=recv_sem, device_id=device, device_id_type=MESH
    )


class Exchange:
    def __init__(self, n, place, device_of, buffers):
        self.n, self.place, self.device_of = n, place, device_of
        self.src, self.dst, self.send_sem, self.recv_sem = buffers

    def start(self):
        @pl.loop(1, self.n)
        def _(offset):
            p = (self.place + offset) & (self.n - 1)
            remote(
                self.src.at[p], self.dst.at[self.place], self.send_sem.at[0], self.recv_sem.at[0], self.device_of(p)
            ).start()

        self.dst[self.place] = self.src[self.place]

    def _all(self):
        part = pl.ds(0, self.n - 1)
        p = (self.place + 1) & (self.n - 1)
        return remote(self.src.at[part], self.dst.at[part], self.send_sem.at[0], self.recv_sem.at[0], self.device_of(p))

    def wait_recv(self):
        self._all().wait_recv()

    def wait_send(self):
        self._all().wait_send()


def picking(source, n):
    return (lax.broadcasted_iota(jnp.int32, (source.shape[0], n), 1) == source).astype(F32).astype(BF16)


def swap_rows(outer, inner, rows):
    n = outer * inner
    row = lax.broadcasted_iota(jnp.int32, (n, 1), 0)
    matrix = picking(lax.rem(row, outer) * inner + row // outer, n)
    return jnp.dot(matrix, rows, preferred_element_type=F32).astype(BF16)


def slot_matrix(routes_ref, live_ref, ndp, capacity):
    count = routes_ref.shape[1]
    row = lax.broadcasted_iota(jnp.int32, (count, count), 0)
    col = lax.broadcasted_iota(jnp.int32, (count, count), 1)
    target = routes_ref[...]
    wide = jnp.broadcast_to(target, (count, count))
    tall = jnp.sum(jnp.where(row == col, wide, 0), axis=1, keepdims=True)
    rank = jnp.sum(((tall == wide) & (row < col)).astype(jnp.int32), axis=0, keepdims=True)
    alive = lax.broadcasted_iota(jnp.int32, (1, count), 1) < live_ref[...]
    slot = jnp.where(alive, rank * ndp + target, -1)
    return (lax.broadcasted_iota(jnp.int32, (ndp * capacity, count), 0) == slot).astype(F32)


def dot_t(left, right):
    return lax.dot_general(left, right, (((1,), (1,)), ((), ())), preferred_element_type=F32)


def t_dot(left, right):
    return lax.dot_general(left, right, (((0,), (0,)), ((), ())), preferred_element_type=F32)


def tiles(total, size, body, start=0):
    @pl.loop(0, total // size)
    def _(i):
        body(pl.ds(pl.multiple_of(start + i * size, size), size))


class Route:
    def __init__(self, z_first, over_z, over_j):
        self.z_first = z_first
        self.nz, self.nj = over_z.n, over_j.n
        self.first, self.second = (over_z, over_j) if z_first else (over_j, over_z)

    def _send(self, exchange, rows):
        exchange.src[...] = rows.reshape(exchange.src.shape)
        exchange.start()

    def _got(self, exchange):
        exchange.wait_recv()
        shape = exchange.dst.shape
        return exchange.dst[...].reshape(shape[0] * shape[1], shape[2])

    def start(self, rows):
        self._send(self.first, rows if self.z_first else swap_rows(self.nz, self.nj, rows))

    def middle(self):
        a, b = (self.nz, self.nj) if self.z_first else (self.nj, self.nz)
        self._send(self.second, swap_rows(a, b, self._got(self.first)))

    def finish(self):
        rows = self._got(self.second)
        return swap_rows(self.nj, self.nz, rows) if self.z_first else rows

    def wait_send(self):
        self.first.wait_send()
        self.second.wait_send()


def kernel(ndp, names, *refs):
    r = SimpleNamespace(**dict(zip(names, refs)))
    me, t = lax.axis_index("dp"), lax.axis_index("tensor")
    nz = ndp // GROUP
    z, j = me // GROUP, lax.rem(me, GROUP)
    y, xl, core = j // 4, lax.rem(j // 2, 2), lax.rem(j, 2)
    z_device = lambda p: {"dp": p * GROUP + j}
    j_device = lambda p: {"dp": z * GROUP + p}
    y_device = lambda p: {"dp": z * GROUP + p * 4 + xl * 2 + core}
    x_device = {"dp": me + 2 - 4 * xl}
    sibling = {"dp": me + 1 - 2 * core}
    partner = {"dp": me + 2 - 4 * xl, "tensor": 1 - t}
    width = r.source.shape[1]
    units = r.win.shape[1]
    half = units // 2
    wide = width // 2
    halves = [slice(0, wide), slice(wide, width)]

    load_cot = pltpu.make_async_copy(r.cotangent, r.cot, r.load_sem.at[2])
    load_in = pltpu.make_async_copy(r.weight_in, r.win, r.load_sem.at[0])
    load_out = pltpu.make_async_copy(r.weight_out, r.wout, r.load_sem.at[1])
    load_cot.start()
    load_in.start()
    load_out.start()

    barrier = pltpu.get_barrier_semaphore()

    @pl.loop(1, nz)
    def _(offset):
        pl.semaphore_signal(barrier, inc=1, device_id=z_device(lax.rem(z + offset, nz)), device_id_type=MESH)

    @pl.loop(1, GROUP)
    def _(offset):
        pl.semaphore_signal(barrier, inc=1, device_id=j_device(lax.rem(j + offset, GROUP)), device_id_type=MESH)

    pl.semaphore_signal(barrier, inc=1, device_id=partner, device_id_type=MESH)

    def exchange(name, n, place, device_of):
        return Exchange(n, place, device_of, tuple(getattr(r, name + end) for end in ("_out", "_in", "_ss", "_rs")))

    def routed(name, z_first):
        return Route(z_first, exchange(name + "z", nz, z, z_device), exchange(name + "j", GROUP, j, j_device))

    def one_way(name, slot, device, part=None):
        out, land, ss, rs = (getattr(r, name + end) for end in ("_out", "_in", "_ss", "_rs"))
        index, sem = (slot, slot) if part is None else ((slot, slice(None), halves[part]), 2 * slot + part)
        return remote(out.at[index], land.at[index], ss.at[sem], rs.at[sem], device)

    r.gain_row[...] = r.gain[...].reshape(1, -1)
    hot = slot_matrix(r.routes, r.live, ndp, 2)
    r.hot[...] = hot.astype(BF16)
    first = lax.broadcasted_iota(jnp.int32, (ndp, width), 1) == 0

    def outgoing(rank):
        part = hot[rank * ndp : (rank + 1) * ndp]
        empty = jnp.sum(part, axis=1, keepdims=True) < 0.5
        rows = jnp.dot(part.astype(BF16), r.source[...], preferred_element_type=F32)
        return jnp.where(empty & first, ABSENT, rows).astype(BF16)

    there = [routed("a" + str(i), i < 2) for i in range(4)]
    leaving = outgoing(0)
    load_cot.wait()
    cot_copy = remote(r.cot, r.cot_in, r.cot_sem.at[0], r.cot_sem.at[1], partner)
    pl.semaphore_wait(barrier, nz + GROUP - 1)
    cot_copy.start()
    there[0].start(leaving[:, halves[0]])
    there[1].start(leaving[:, halves[1]])
    leaving = outgoing(1)
    there[2].start(leaving[:, halves[0]])
    there[3].start(leaving[:, halves[1]])

    strip = width // (nz * 8)
    step = width // RING

    def turn(side, rows):
        @pl.loop(0, RING)
        def _(i):
            row = lax.broadcasted_iota(jnp.int32, (step, 1), 0)
            x_at, z_at, rest = row // (step // 2), lax.rem(row // strip, nz), lax.rem(row, strip)
            pick = picking((z_at * 8 + i * 2 + x_at) * strip + rest, width)
            at = pl.ds(pl.multiple_of(i * step, step), step)
            r.turned[at, side * 2 * ndp : (side + 1) * 2 * ndp] = dot_t(pick, rows).astype(BF16)

    def order_cot(side, rows):
        rows = swap_rows(ndp, 2, rows)
        r.cots[side * 2 * ndp : (side + 1) * 2 * ndp] = rows
        turn(side, rows)

    order_cot(0, r.cot[...])
    there[0].middle()
    there[2].middle()
    load_in.wait()
    load_out.wait()

    def process(k):
        c = k % 2
        rows = pl.ds(k * ndp, ndp)
        slots = (r.fr_out if k < 2 else r.fr_in)[c].astype(F32)
        present = slots[:, :1] < 0.5 * ABSENT
        frames = jnp.where(present, slots, 0.0)
        centred = frames - jnp.mean(frames, axis=1, keepdims=True)
        inv_std = lax.rsqrt(jnp.mean(centred * centred, axis=1, keepdims=True) + epsilon)
        normed = centred * inv_std
        if k < 2:
            r.normed[c] = normed
            r.inv_std[c] = inv_std
        r.scaled[...] = (normed * r.gain_row[...]).astype(BF16)
        r.grads[rows] = jnp.where(present, r.cots[rows].astype(F32), 0.0).astype(BF16)

        def tile(n):
            hidden = jnp.dot(r.scaled[...], r.win[:, n], preferred_element_type=F32)
            grad_act = 0.5 * dot_t(r.grads[rows], r.wout[n, :])
            gate = jax.nn.sigmoid(hidden)
            r.act[rows, n] = jnp.where(present, hidden * gate, 0.0).astype(BF16)
            r.gh[rows, n] = (grad_act * gate * (1.0 + hidden * (1.0 - gate))).astype(BF16)

        tiles(units, 768, tile)

    def scaled_grad(k, out, c, start=0, length=None):
        def tile(n):
            out[c, :, n] = dot_t(r.gh[pl.ds(k * ndp, ndp), :], r.win[n, :]).astype(BF16)

        tiles(length or width, 768, tile, start)

    def mix(k, out, c):
        def tile(n):
            out[c, :, n] = jnp.dot(
                r.act[pl.ds(k * ndp, ndp), :], r.wout[:, n], preferred_element_type=F32
            ).astype(BF16)

        tiles(width, 768, tile)

    frames_over = [one_way("fr", i // 2, partner, i % 2) for i in range(4)]

    def land(i):
        r.fr_out[i // 2, :, halves[i % 2]] = there[i].finish()
        frames_over[i].start()

    there[1].middle()
    there[3].middle()
    land(0)
    land(1)
    process(0)
    scaled_grad(0, r.gs_own, 0)
    cot_copy.wait_recv()
    order_cot(1, r.cot_in[...])
    land(2)
    land(3)
    process(1)
    frames_over[0].wait_recv()
    frames_over[1].wait_recv()
    process(2)
    sums = [one_way("gs", i // 2, partner, i % 2) for i in range(4)]
    scaled_grad(2, r.gs_out, 0)
    scaled_grad(1, r.gs_own, 1)
    mix(0, r.mx_own, 0)
    frames_over[2].wait_recv()
    frames_over[3].wait_recv()
    sums[0].start()
    sums[1].start()
    process(3)

    up, down, opposite = lax.rem(y + 1, RING), lax.rem(y + 3, RING), lax.rem(y + 2, RING)
    order = [opposite, up, down, y]

    def product(y_at, which):
        columns = pl.ds(pl.multiple_of(which * half, half), half)
        left = r.turned[pl.ds(pl.multiple_of(y_at * step, step), step), :]
        return (0.5 * jnp.dot(left, r.act[:, columns], preferred_element_type=F32)).reshape(2, step // 2, half)

    def to_sibling(i):
        part = pl.ds(2 * order[i], 2)
        return remote(r.sib_out.at[part], r.sib_in.at[part], r.sib_ss.at[i], r.sib_rs.at[i], sibling)

    for i in range(4):
        r.sib_out[pl.ds(2 * order[i], 2)] = product(order[i], 1 - core).astype(BF16)
        to_sibling(i).start()
    for part in range(2):
        scaled_grad(3, r.gs_out, 1, part * wide, wide)
        sums[2 + part].start()

    def keep(i):
        r.mine[pl.ds(2 * order[i], 2)] = product(order[i], core)
        to_sibling(i).wait_recv()

    block = half // 2
    blocks = [slice(0, block), slice(block, half)]
    part_rows = step // 4

    def cores(y_at, x_at, b):
        p = y_at * 2 + x_at
        return r.mine[p, :, blocks[b]] + r.sib_in[p, :, blocks[b]].astype(F32)

    def ring1(name, slot):
        return one_way(name, slot, y_device(down) if slot else y_device(up))

    def ring2(name, slot):
        return one_way(name, slot, y_device(down) if slot // 2 else y_device(up))

    def send(copy, buffer, index, value):
        buffer[index] = value.astype(BF16)
        copy.start()

    def x_first(i):
        return remote(r.bx_out.at[i], r.bx_in.at[i], r.bx_ss.at[i], r.bx_rs.at[i], x_device)

    keep(0)
    send(x_first(0), r.bx_out, 0, cores(opposite, 1 - xl, 1))
    for s in range(2):
        send(ring1("a1", s), r.a1_out, s, cores(opposite, s, 0))
    keep(1)
    send(x_first(1), r.bx_out, 1, cores(up, 1 - xl, 1))
    send(ring2("a2", 1), r.a2_out, 1, cores(up, 1, 0))
    keep(2)
    send(x_first(2), r.bx_out, 2, cores(down, 1 - xl, 1))
    send(ring2("a2", 2), r.a2_out, 2, cores(down, 0, 0))
    keep(3)
    send(x_first(3), r.bx_out, 3, cores(y, 1 - xl, 1))

    def gradient(c):
        normed = r.normed[c]
        g = (r.gs_own[c].astype(F32) + r.gs_in[c].astype(F32)) * r.gain_row[...]
        first_mean = jnp.mean(g, axis=1, keepdims=True)
        second_mean = jnp.mean(g * normed, axis=1, keepdims=True)
        own = r.grads[pl.ds(c * ndp, ndp)].astype(F32)
        return (own + r.inv_std[c] * (g - first_mean - normed * second_mean)).astype(BF16)

    back = [routed("b" + str(i), i < 2) for i in range(4)]

    def give(c):
        sums[2 * c].wait_recv()
        sums[2 * c + 1].wait_recv()
        rows = gradient(c)
        back[2 * c].start(rows[:, halves[0]])
        back[2 * c + 1].start(rows[:, halves[1]])

    give(0)
    ring1("a1", 0).wait_recv()
    send(ring2("a2", 0), r.a2_out, 0, cores(up, 0, 0) + r.a1_in[0].astype(F32))
    ring1("a1", 1).wait_recv()
    send(ring2("a2", 3), r.a2_out, 3, cores(down, 1, 0) + r.a1_in[1].astype(F32))

    def summed(i):
        r.bsum[i] = cores(order[i], xl, 1) + r.bx_in[i].astype(F32)

    x_first(0).wait_recv()
    summed(0)
    for s in range(2):
        send(ring1("b1", s), r.b1_out, s, r.bsum[0, s * part_rows : (s + 1) * part_rows])
    x_first(1).wait_recv()
    summed(1)
    send(ring2("b2", 1), r.b2_out, 1, r.bsum[1, part_rows:])
    give(1)
    x_first(2).wait_recv()
    summed(2)
    send(ring2("b2", 2), r.b2_out, 2, r.bsum[2, :part_rows])
    mixes = [one_way("mx", c, partner) for c in range(2)]
    mix(2, r.mx_out, 0)
    mixes[0].start()
    ring1("b1", 0).wait_recv()
    send(ring2("b2", 0), r.b2_out, 0, r.bsum[1, :part_rows] + r.b1_in[0].astype(F32))
    ring1("b1", 1).wait_recv()
    send(ring2("b2", 3), r.b2_out, 3, r.bsum[2, part_rows:] + r.b1_in[1].astype(F32))
    for slot in range(4):
        ring2("a2", slot).wait_recv()
    for s in range(2):
        r.total[s] = cores(y, s, 0) + r.a2_in[s].astype(F32) + r.a2_in[2 + s].astype(F32)
    r.ax_out[...] = r.total[1 - xl].astype(BF16)
    x_last = remote(r.ax_out, r.ax_in, r.ax_ss.at[0], r.ax_rs.at[0], x_device)
    x_last.start()
    back[2].middle()
    back[3].middle()
    mix(3, r.mx_out, 1)
    mixes[1].start()
    x_first(3).wait_recv()
    summed(3)
    for slot in range(4):
        ring2("b2", slot).wait_recv()
    over_z = [exchange("s" + str(b), nz, z, z_device) for b in range(2)]
    for s in range(2):
        at = slice(s * part_rows, (s + 1) * part_rows)
        r.bsum[3, at] = r.bsum[3, at] + r.b2_in[s].astype(F32) + r.b2_in[2 + s].astype(F32)
    r.s1_out[...] = r.bsum[3].astype(BF16).reshape(r.s1_out.shape)
    over_z[1].start()
    x_last.wait_recv()
    r.s0_out[...] = (r.total[xl] + r.ax_in[...].astype(F32)).astype(BF16).reshape(r.s0_out.shape)
    over_z[0].start()
    back[0].middle()
    back[1].middle()
    mix(1, r.mx_own, 1)
    x_last.wait_send()
    cot_copy.wait_send()
    for copy in sums + frames_over + there:
        copy.wait_send()
    for name in ("a", "b"):
        for slot in range(2):
            ring1(name + "1", slot).wait_send()
        for slot in range(4):
            ring2(name + "2", slot).wait_send()
    for i in range(4):
        to_sibling(i).wait_send()
        x_first(i).wait_send()

    r.rows[0, :, halves[0]] = back[0].finish()
    r.rows[0, :, halves[1]] = back[1].finish()
    for b in (1, 0):
        over_z[b].wait_recv()
        r.last_out[:, blocks[b]] = jnp.sum((r.s0_in, r.s1_in)[b][...].astype(F32), axis=0)
    last = remote(r.last_out, r.last_in, r.last_sem.at[0], r.last_sem.at[1], sibling)
    last.start()
    for c in range(2):
        mixes[c].wait_recv()
    mixed_rows = []
    for c in range(2):
        slots = r.fr_out[c].astype(F32)
        frames = jnp.where(slots[:, :1] < 0.5 * ABSENT, slots, 0.0)
        mixed_rows.append((frames + 0.5 * (r.mx_own[c].astype(F32) + r.mx_in[c].astype(F32))).astype(BF16))
    r.mixed[...] = swap_rows(2, ndp, jnp.concatenate(mixed_rows, axis=0))
    r.rows[1, :, halves[0]] = back[2].finish()
    r.rows[1, :, halves[1]] = back[3].finish()
    r.grad_source[...] = (t_dot(r.hot[:ndp], r.rows[0]) + t_dot(r.hot[ndp:], r.rows[1])).astype(BF16)

    last.wait_recv()
    own, other = r.last_out[...], r.last_in[...]
    count = own.shape[0] // 2
    is_low = core == 0
    own = jnp.where(is_low, own[:count], own[count:])
    other = jnp.where(is_low, other[:count], other[count:])
    r.grad_out[:, :half] = jnp.where(is_low, own, other)
    r.grad_out[:, half:] = jnp.where(is_low, other, own)

    last.wait_send()
    for copy in mixes + back + over_z:
        copy.wait_send()


def finish_kernel(mixed, grad_source, grad_out, mixed_out, grad_source_out, grad_out_out):
    mixed_out[...] = mixed[...]
    grad_source_out[...] = grad_source[...]
    grad_out_out[...] = grad_out[...]


def local(source_frames, routes, live_frames, norm_gain, weight_in, weight_out, cotangent):
    ndp = lax.axis_size("dp")
    nz = ndp // GROUP
    width, units = weight_in.shape
    half, strip = units // 2, width // ndp * 2
    block, tall = half // 2, width // 8
    vmem = pltpu.VMEM
    inputs = {
        "source": source_frames,
        "routes": routes.reshape(1, -1),
        "live": live_frames.reshape(1, 1),
        "gain": norm_gain,
        "cotangent": cotangent,
        "weight_in": weight_in,
        "weight_out": weight_out,
    }
    outputs = {
        "mixed": jax.ShapeDtypeStruct(cotangent.shape, BF16),
        "grad_source": jax.ShapeDtypeStruct(source_frames.shape, BF16),
        "grad_out": jax.ShapeDtypeStruct((width // ndp, units), F32),
    }
    scratch = {
        "win": vmem(weight_in.shape, BF16),
        "wout": vmem(weight_out.shape, BF16),
        "cot": vmem(cotangent.shape, BF16),
        "cot_in": vmem(cotangent.shape, BF16),
        "cot_sem": DMA((2,)),
        "cots": vmem((4 * ndp, width), BF16),
        "load_sem": DMA((3,)),
        "hot": vmem((2 * ndp, source_frames.shape[0]), BF16),
        "turned": vmem((width, 4 * ndp), BF16),
        "grads": vmem((4 * ndp, width), BF16),
        "act": vmem((4 * ndp, units), BF16),
        "gh": vmem((4 * ndp, units), BF16),
        "gain_row": vmem((1, width), F32),
        "scaled": vmem((ndp, width), BF16),
        "normed": vmem((2, ndp, width), F32),
        "inv_std": vmem((2, ndp, 1), F32),
        "gs_own": vmem((2, ndp, width), BF16),
        "mx_own": vmem((2, ndp, width), BF16),
        "rows": vmem((2, ndp, width), BF16),
        "mine": vmem((8, tall, half), F32),
        "total": vmem((2, tall, block), F32),
        "bsum": vmem((4, tall, block), F32),
        "last_out": vmem((strip, half), F32),
        "last_in": vmem((strip, half), F32),
        "last_sem": DMA((2,)),
    }

    def both_ways(name, shape, count):
        scratch[name + "_out"] = vmem(shape, BF16)
        scratch[name + "_in"] = vmem(shape, BF16)
        scratch[name + "_ss"] = DMA((count,))
        scratch[name + "_rs"] = DMA((count,))

    for prefix in "ab":
        for i in "0123":
            both_ways(prefix + i + "z", (nz, GROUP, width // 2), 1)
            both_ways(prefix + i + "j", (GROUP, nz, width // 2), 1)
    for name, count in (("fr", 4), ("gs", 4), ("mx", 2)):
        both_ways(name, (2, ndp, width), count)
    both_ways("sib", (8, tall, half), 4)
    both_ways("a1", (2, tall, block), 2)
    both_ways("a2", (4, tall, block), 4)
    both_ways("b1", (2, tall // 2, block), 2)
    both_ways("b2", (4, tall // 2, block), 4)
    both_ways("ax", (tall, block), 1)
    both_ways("bx", (4, tall, block), 4)
    both_ways("s0", (nz, strip, block), 1)
    both_ways("s1", (nz, strip, block), 1)

    in_vmem = pl.BlockSpec(memory_space=pltpu.VMEM)
    anywhere = pl.BlockSpec(memory_space=pl.ANY)
    from_hbm = ("weight_in", "weight_out", "cotangent")
    results = pl.pallas_call(
        functools.partial(kernel, ndp, list(inputs) + list(outputs) + list(scratch)),
        out_shape=list(outputs.values()),
        in_specs=[anywhere if name in from_hbm else in_vmem for name in inputs],
        out_specs=[in_vmem] * 3,
        scratch_shapes=list(scratch.values()),
        compiler_params=pltpu.CompilerParams(
            collective_id=1, has_side_effects=True, vmem_limit_bytes=60 * 1024 * 1024
        ),
        name="module",
    )(*inputs.values())
    mixed, grad_source, grad_out = pl.pallas_call(
        finish_kernel,
        out_shape=list(outputs.values()),
        in_specs=[in_vmem] * 3,
        out_specs=[in_vmem] * 3,
        name="finish",
    )(*results)
    return (mixed, grad_source, grad_out.T)


def solution(mesh):
    return jax.shard_map(
        local,
        mesh=mesh,
        in_specs=(
            P(("dp", "tensor"), None),
            P(("dp", "tensor"), None),
            P(("dp", "tensor")),
            P(),
            P(None, "tensor"),
            P("tensor", None),
            P(("dp", "tensor"), None),
        ),
        out_specs=(P(("dp", "tensor"), None), P(("dp", "tensor"), None), P("tensor", "dp")),
        check_vma=False,
    )
```

```python
import functools
from types import SimpleNamespace

import jax
import jax.numpy as jnp
from jax import lax
from jax.experimental import pallas as pl
from jax.experimental.pallas import tpu as pltpu
from jax.sharding import PartitionSpec as P

epsilon = 1e-05
ABSENT = 64.0
MESH = pl.DeviceIdType.MESH
GROUP = 16
RING = 4
DMA = pltpu.SemaphoreType.DMA
BF16, F32 = jnp.bfloat16, jnp.float32


def remote(src, dst, send_sem, recv_sem, device):
    return pltpu.make_async_remote_copy(
        src_ref=src, dst_ref=dst, send_sem=send_sem, recv_sem=recv_sem, device_id=device, device_id_type=MESH
    )


class Exchange:
    def __init__(self, n, place, device_of, buffers):
        self.n, self.place, self.device_of = n, place, device_of
        self.src, self.dst, self.send_sem, self.recv_sem = buffers

    def start(self):
        @pl.loop(1, self.n)
        def _(offset):
            p = (self.place + offset) & (self.n - 1)
            remote(
                self.src.at[p], self.dst.at[self.place], self.send_sem.at[0], self.recv_sem.at[0], self.device_of(p)
            ).start()

        self.dst[self.place] = self.src[self.place]

    def _all(self):
        part = pl.ds(0, self.n - 1)
        p = (self.place + 1) & (self.n - 1)
        return remote(self.src.at[part], self.dst.at[part], self.send_sem.at[0], self.recv_sem.at[0], self.device_of(p))

    def wait_recv(self):
        self._all().wait_recv()

    def wait_send(self):
        self._all().wait_send()


def picking(source, n):
    return (lax.broadcasted_iota(jnp.int32, (source.shape[0], n), 1) == source).astype(F32).astype(BF16)


def swap_rows(outer, inner, rows):
    n = outer * inner
    row = lax.broadcasted_iota(jnp.int32, (n, 1), 0)
    matrix = picking(lax.rem(row, outer) * inner + row // outer, n)
    return jnp.dot(matrix, rows, preferred_element_type=F32).astype(BF16)


def slot_matrix(routes_ref, live_ref, ndp, capacity):
    count = routes_ref.shape[1]
    row = lax.broadcasted_iota(jnp.int32, (count, count), 0)
    col = lax.broadcasted_iota(jnp.int32, (count, count), 1)
    target = routes_ref[...]
    wide = jnp.broadcast_to(target, (count, count))
    tall = jnp.sum(jnp.where(row == col, wide, 0), axis=1, keepdims=True)
    rank = jnp.sum(((tall == wide) & (row < col)).astype(jnp.int32), axis=0, keepdims=True)
    alive = lax.broadcasted_iota(jnp.int32, (1, count), 1) < live_ref[...]
    slot = jnp.where(alive, rank * ndp + target, -1)
    return (lax.broadcasted_iota(jnp.int32, (ndp * capacity, count), 0) == slot).astype(F32)


def dot_t(left, right):
    return lax.dot_general(left, right, (((1,), (1,)), ((), ())), preferred_element_type=F32)


def t_dot(left, right):
    return lax.dot_general(left, right, (((0,), (0,)), ((), ())), preferred_element_type=F32)


def tiles(total, size, body, start=0):
    @pl.loop(0, total // size)
    def _(i):
        body(pl.ds(pl.multiple_of(start + i * size, size), size))


class Route:
    def __init__(self, z_first, over_z, over_j):
        self.z_first = z_first
        self.nz, self.nj = over_z.n, over_j.n
        self.first, self.second = (over_z, over_j) if z_first else (over_j, over_z)

    def _send(self, exchange, rows):
        exchange.src[...] = rows.reshape(exchange.src.shape)
        exchange.start()

    def _got(self, exchange):
        exchange.wait_recv()
        shape = exchange.dst.shape
        return exchange.dst[...].reshape(shape[0] * shape[1], shape[2])

    def start(self, rows):
        self._send(self.first, rows if self.z_first else swap_rows(self.nz, self.nj, rows))

    def middle(self):
        a, b = (self.nz, self.nj) if self.z_first else (self.nj, self.nz)
        self._send(self.second, swap_rows(a, b, self._got(self.first)))

    def finish(self):
        rows = self._got(self.second)
        return swap_rows(self.nj, self.nz, rows) if self.z_first else rows

    def wait_send(self):
        self.first.wait_send()
        self.second.wait_send()


def kernel(ndp, names, *refs):
    r = SimpleNamespace(**dict(zip(names, refs)))
    me, t = lax.axis_index("dp"), lax.axis_index("tensor")
    nz = ndp // GROUP
    z, j = me // GROUP, lax.rem(me, GROUP)
    y, xl, core = j // 4, lax.rem(j // 2, 2), lax.rem(j, 2)
    z_device = lambda p: {"dp": p * GROUP + j}
    j_device = lambda p: {"dp": z * GROUP + p}
    y_device = lambda p: {"dp": z * GROUP + p * 4 + xl * 2 + core}
    x_device = {"dp": me + 2 - 4 * xl}
    sibling = {"dp": me + 1 - 2 * core}
    partner = {"dp": me + 2 - 4 * xl, "tensor": 1 - t}
    width = r.source.shape[1]
    units = r.win.shape[1]
    half = units // 2
    wide = width // 2
    halves = [slice(0, wide), slice(wide, width)]

    load_cot = pltpu.make_async_copy(r.cotangent, r.cot, r.load_sem.at[2])
    load_in = pltpu.make_async_copy(r.weight_in, r.win, r.load_sem.at[0])
    load_out = pltpu.make_async_copy(r.weight_out, r.wout, r.load_sem.at[1])
    load_cot.start()
    load_in.start()
    load_out.start()

    barrier = pltpu.get_barrier_semaphore()

    @pl.loop(1, nz)
    def _(offset):
        pl.semaphore_signal(barrier, inc=1, device_id=z_device(lax.rem(z + offset, nz)), device_id_type=MESH)

    @pl.loop(1, GROUP)
    def _(offset):
        pl.semaphore_signal(barrier, inc=1, device_id=j_device(lax.rem(j + offset, GROUP)), device_id_type=MESH)

    pl.semaphore_signal(barrier, inc=1, device_id=partner, device_id_type=MESH)

    def exchange(name, n, place, device_of):
        return Exchange(n, place, device_of, tuple(getattr(r, name + end) for end in ("_out", "_in", "_ss", "_rs")))

    def routed(name, z_first):
        return Route(z_first, exchange(name + "z", nz, z, z_device), exchange(name + "j", GROUP, j, j_device))

    def one_way(name, slot, device, part=None):
        out, land, ss, rs = (getattr(r, name + end) for end in ("_out", "_in", "_ss", "_rs"))
        index, sem = (slot, slot) if part is None else ((slot, slice(None), halves[part]), 2 * slot + part)
        return remote(out.at[index], land.at[index], ss.at[sem], rs.at[sem], device)

    r.gain_row[...] = r.gain[...].reshape(1, -1)
    hot = slot_matrix(r.routes, r.live, ndp, 2)
    r.hot[...] = hot.astype(BF16)
    first = lax.broadcasted_iota(jnp.int32, (ndp, width), 1) == 0

    def outgoing(rank):
        part = hot[rank * ndp : (rank + 1) * ndp]
        empty = jnp.sum(part, axis=1, keepdims=True) < 0.5
        rows = jnp.dot(part.astype(BF16), r.source[...], preferred_element_type=F32)
        return jnp.where(empty & first, ABSENT, rows).astype(BF16)

    there = [routed("a" + str(i), i < 2) for i in range(4)]
    leaving = outgoing(0)
    load_cot.wait()
    cot_copy = remote(r.cot, r.cot_in, r.cot_sem.at[0], r.cot_sem.at[1], partner)
    pl.semaphore_wait(barrier, nz + GROUP - 1)
    cot_copy.start()
    there[0].start(leaving[:, halves[0]])
    there[1].start(leaving[:, halves[1]])
    leaving = outgoing(1)
    there[2].start(leaving[:, halves[0]])
    there[3].start(leaving[:, halves[1]])

    strip = width // (nz * 8)
    step = width // RING

    def turn(side, rows):
        @pl.loop(0, RING)
        def _(i):
            row = lax.broadcasted_iota(jnp.int32, (step, 1), 0)
            x_at, z_at, rest = row // (step // 2), lax.rem(row // strip, nz), lax.rem(row, strip)
            pick = picking((z_at * 8 + i * 2 + x_at) * strip + rest, width)
            at = pl.ds(pl.multiple_of(i * step, step), step)
            r.turned[at, side * 2 * ndp : (side + 1) * 2 * ndp] = dot_t(pick, rows).astype(BF16)

    def order_cot(side, rows):
        rows = swap_rows(ndp, 2, rows)
        r.cots[side * 2 * ndp : (side + 1) * 2 * ndp] = rows
        turn(side, rows)

    order_cot(0, r.cot[...])
    there[0].middle()
    there[2].middle()
    load_in.wait()
    load_out.wait()

    def process(k):
        c = k % 2
        rows = pl.ds(k * ndp, ndp)
        slots = (r.fr_out if k < 2 else r.fr_in)[c].astype(F32)
        present = slots[:, :1] < 0.5 * ABSENT
        frames = jnp.where(present, slots, 0.0)
        centred = frames - jnp.mean(frames, axis=1, keepdims=True)
        inv_std = lax.rsqrt(jnp.mean(centred * centred, axis=1, keepdims=True) + epsilon)
        normed = centred * inv_std
        if k < 2:
            r.normed[c] = normed
            r.inv_std[c] = inv_std
        r.scaled[...] = (normed * r.gain_row[...]).astype(BF16)
        r.grads[rows] = jnp.where(present, r.cots[rows].astype(F32), 0.0).astype(BF16)

        def tile(n):
            hidden = jnp.dot(r.scaled[...], r.win[:, n], preferred_element_type=F32)
            grad_act = 0.5 * dot_t(r.grads[rows], r.wout[n, :])
            gate = jax.nn.sigmoid(hidden)
            r.act[rows, n] = jnp.where(present, hidden * gate, 0.0).astype(BF16)
            r.gh[rows, n] = (grad_act * gate * (1.0 + hidden * (1.0 - gate))).astype(BF16)

        tiles(units, 768, tile)

    def scaled_grad(k, out, c, start=0, length=None):
        def tile(n):
            out[c, :, n] = dot_t(r.gh[pl.ds(k * ndp, ndp), :], r.win[n, :]).astype(BF16)

        tiles(length or width, 768, tile, start)

    def mix(k, out, c):
        def tile(n):
            out[c, :, n] = jnp.dot(
                r.act[pl.ds(k * ndp, ndp), :], r.wout[:, n], preferred_element_type=F32
            ).astype(BF16)

        tiles(width, 768, tile)

    frames_over = [one_way("fr", i // 2, partner, i % 2) for i in range(4)]

    def land(i):
        r.fr_out[i // 2, :, halves[i % 2]] = there[i].finish()
        frames_over[i].start()

    there[1].middle()
    there[3].middle()
    land(0)
    land(1)
    process(0)
    scaled_grad(0, r.gs_own, 0)
    cot_copy.wait_recv()
    order_cot(1, r.cot_in[...])
    land(2)
    land(3)
    process(1)
    frames_over[0].wait_recv()
    frames_over[1].wait_recv()
    process(2)
    sums = [one_way("gs", i // 2, partner, i % 2) for i in range(4)]
    scaled_grad(2, r.gs_out, 0)
    scaled_grad(1, r.gs_own, 1)
    mix(0, r.mx_own, 0)
    frames_over[2].wait_recv()
    frames_over[3].wait_recv()
    sums[0].start()
    sums[1].start()
    process(3)

    up, down, opposite = lax.rem(y + 1, RING), lax.rem(y + 3, RING), lax.rem(y + 2, RING)
    order = [opposite, up, down, y]

    def product(y_at, which):
        columns = pl.ds(pl.multiple_of(which * half, half), half)
        left = r.turned[pl.ds(pl.multiple_of(y_at * step, step), step), :]
        return (0.5 * jnp.dot(left, r.act[:, columns], preferred_element_type=F32)).reshape(2, step // 2, half)

    def to_sibling(i):
        part = pl.ds(2 * order[i], 2)
        return remote(r.sib_out.at[part], r.sib_in.at[part], r.sib_ss.at[i], r.sib_rs.at[i], sibling)

    for i in range(4):
        r.sib_out[pl.ds(2 * order[i], 2)] = product(order[i], 1 - core).astype(BF16)
        to_sibling(i).start()
    for part in range(2):
        scaled_grad(3, r.gs_out, 1, part * wide, wide)
        sums[2 + part].start()

    def keep(i):
        r.mine[pl.ds(2 * order[i], 2)] = product(order[i], core)
        to_sibling(i).wait_recv()

    block = half // 2
    blocks = [slice(0, block), slice(block, half)]
    part_rows = step // 4

    def cores(y_at, x_at, b):
        p = y_at * 2 + x_at
        return r.mine[p, :, blocks[b]] + r.sib_in[p, :, blocks[b]].astype(F32)

    def ring1(name, slot):
        return one_way(name, slot, y_device(down) if slot else y_device(up))

    def ring2(name, slot):
        return one_way(name, slot, y_device(down) if slot // 2 else y_device(up))

    def send(copy, buffer, index, value):
        buffer[index] = value.astype(BF16)
        copy.start()

    def x_first(i):
        return remote(r.bx_out.at[i], r.bx_in.at[i], r.bx_ss.at[i], r.bx_rs.at[i], x_device)

    keep(0)
    send(x_first(0), r.bx_out, 0, cores(opposite, 1 - xl, 1))
    for s in range(2):
        send(ring1("a1", s), r.a1_out, s, cores(opposite, s, 0))
    keep(1)
    send(x_first(1), r.bx_out, 1, cores(up, 1 - xl, 1))
    send(ring2("a2", 1), r.a2_out, 1, cores(up, 1, 0))
    keep(2)
    send(x_first(2), r.bx_out, 2, cores(down, 1 - xl, 1))
    send(ring2("a2", 2), r.a2_out, 2, cores(down, 0, 0))
    keep(3)
    send(x_first(3), r.bx_out, 3, cores(y, 1 - xl, 1))

    def gradient(c):
        normed = r.normed[c]
        g = (r.gs_own[c].astype(F32) + r.gs_in[c].astype(F32)) * r.gain_row[...]
        first_mean = jnp.mean(g, axis=1, keepdims=True)
        second_mean = jnp.mean(g * normed, axis=1, keepdims=True)
        own = r.grads[pl.ds(c * ndp, ndp)].astype(F32)
        return (own + r.inv_std[c] * (g - first_mean - normed * second_mean)).astype(BF16)

    back = [routed("b" + str(i), i < 2) for i in range(4)]

    def give(c):
        sums[2 * c].wait_recv()
        sums[2 * c + 1].wait_recv()
        rows = gradient(c)
        back[2 * c].start(rows[:, halves[0]])
        back[2 * c + 1].start(rows[:, halves[1]])

    give(0)
    ring1("a1", 0).wait_recv()
    send(ring2("a2", 0), r.a2_out, 0, cores(up, 0, 0) + r.a1_in[0].astype(F32))
    ring1("a1", 1).wait_recv()
    send(ring2("a2", 3), r.a2_out, 3, cores(down, 1, 0) + r.a1_in[1].astype(F32))

    def summed(i):
        r.bsum[i] = cores(order[i], xl, 1) + r.bx_in[i].astype(F32)

    x_first(0).wait_recv()
    summed(0)
    for s in range(2):
        send(ring1("b1", s), r.b1_out, s, r.bsum[0, s * part_rows : (s + 1) * part_rows])
    x_first(1).wait_recv()
    summed(1)
    send(ring2("b2", 1), r.b2_out, 1, r.bsum[1, part_rows:])
    give(1)
    x_first(2).wait_recv()
    summed(2)
    send(ring2("b2", 2), r.b2_out, 2, r.bsum[2, :part_rows])
    mixes = [one_way("mx", c, partner) for c in range(2)]
    mix(2, r.mx_out, 0)
    mixes[0].start()
    ring1("b1", 0).wait_recv()
    send(ring2("b2", 0), r.b2_out, 0, r.bsum[1, :part_rows] + r.b1_in[0].astype(F32))
    ring1("b1", 1).wait_recv()
    send(ring2("b2", 3), r.b2_out, 3, r.bsum[2, part_rows:] + r.b1_in[1].astype(F32))
    for slot in range(4):
        ring2("a2", slot).wait_recv()
    for s in range(2):
        r.total[s] = cores(y, s, 0) + r.a2_in[s].astype(F32) + r.a2_in[2 + s].astype(F32)
    r.ax_out[...] = r.total[1 - xl].astype(BF16)
    x_last = remote(r.ax_out, r.ax_in, r.ax_ss.at[0], r.ax_rs.at[0], x_device)
    x_last.start()
    x_first(3).wait_recv()
    summed(3)
    for slot in range(4):
        ring2("b2", slot).wait_recv()
    over_z = [exchange("s" + str(b), nz, z, z_device) for b in range(2)]
    for s in range(2):
        at = slice(s * part_rows, (s + 1) * part_rows)
        r.bsum[3, at] = r.bsum[3, at] + r.b2_in[s].astype(F32) + r.b2_in[2 + s].astype(F32)
    r.s1_out[...] = r.bsum[3].astype(BF16).reshape(r.s1_out.shape)
    over_z[1].start()
    back[2].middle()
    back[3].middle()
    mix(3, r.mx_out, 1)
    mixes[1].start()
    x_last.wait_recv()
    r.s0_out[...] = (r.total[xl] + r.ax_in[...].astype(F32)).astype(BF16).reshape(r.s0_out.shape)
    over_z[0].start()
    back[0].middle()
    back[1].middle()
    mix(1, r.mx_own, 1)
    x_last.wait_send()
    cot_copy.wait_send()
    for copy in sums + frames_over + there:
        copy.wait_send()
    for name in ("a", "b"):
        for slot in range(2):
            ring1(name + "1", slot).wait_send()
        for slot in range(4):
            ring2(name + "2", slot).wait_send()
    for i in range(4):
        to_sibling(i).wait_send()
        x_first(i).wait_send()

    r.rows[0, :, halves[0]] = back[0].finish()
    r.rows[0, :, halves[1]] = back[1].finish()
    for b in (1, 0):
        over_z[b].wait_recv()
        r.last_out[:, blocks[b]] = jnp.sum((r.s0_in, r.s1_in)[b][...].astype(F32), axis=0)
    last = remote(r.last_out, r.last_in, r.last_sem.at[0], r.last_sem.at[1], sibling)
    last.start()
    for c in range(2):
        mixes[c].wait_recv()
    mixed_rows = []
    for c in range(2):
        slots = r.fr_out[c].astype(F32)
        frames = jnp.where(slots[:, :1] < 0.5 * ABSENT, slots, 0.0)
        mixed_rows.append((frames + 0.5 * (r.mx_own[c].astype(F32) + r.mx_in[c].astype(F32))).astype(BF16))
    r.mixed[...] = swap_rows(2, ndp, jnp.concatenate(mixed_rows, axis=0))
    r.rows[1, :, halves[0]] = back[2].finish()
    r.rows[1, :, halves[1]] = back[3].finish()
    r.grad_source[...] = (t_dot(r.hot[:ndp], r.rows[0]) + t_dot(r.hot[ndp:], r.rows[1])).astype(BF16)

    last.wait_recv()
    own, other = r.last_out[...], r.last_in[...]
    count = own.shape[0] // 2
    is_low = core == 0
    own = jnp.where(is_low, own[:count], own[count:])
    other = jnp.where(is_low, other[:count], other[count:])
    r.grad_out[:, :half] = jnp.where(is_low, own, other)
    r.grad_out[:, half:] = jnp.where(is_low, other, own)

    last.wait_send()
    for copy in mixes + back + over_z:
        copy.wait_send()


def finish_kernel(mixed, grad_source, grad_out, mixed_out, grad_source_out, grad_out_out):
    mixed_out[...] = mixed[...]
    grad_source_out[...] = grad_source[...]
    grad_out_out[...] = grad_out[...]


def local(source_frames, routes, live_frames, norm_gain, weight_in, weight_out, cotangent):
    ndp = lax.axis_size("dp")
    nz = ndp // GROUP
    width, units = weight_in.shape
    half, strip = units // 2, width // ndp * 2
    block, tall = half // 2, width // 8
    vmem = pltpu.VMEM
    inputs = {
        "source": source_frames,
        "routes": routes.reshape(1, -1),
        "live": live_frames.reshape(1, 1),
        "gain": norm_gain,
        "cotangent": cotangent,
        "weight_in": weight_in,
        "weight_out": weight_out,
    }
    outputs = {
        "mixed": jax.ShapeDtypeStruct(cotangent.shape, BF16),
        "grad_source": jax.ShapeDtypeStruct(source_frames.shape, BF16),
        "grad_out": jax.ShapeDtypeStruct((width // ndp, units), F32),
    }
    scratch = {
        "win": vmem(weight_in.shape, BF16),
        "wout": vmem(weight_out.shape, BF16),
        "cot": vmem(cotangent.shape, BF16),
        "cot_in": vmem(cotangent.shape, BF16),
        "cot_sem": DMA((2,)),
        "cots": vmem((4 * ndp, width), BF16),
        "load_sem": DMA((3,)),
        "hot": vmem((2 * ndp, source_frames.shape[0]), BF16),
        "turned": vmem((width, 4 * ndp), BF16),
        "grads": vmem((4 * ndp, width), BF16),
        "act": vmem((4 * ndp, units), BF16),
        "gh": vmem((4 * ndp, units), BF16),
        "gain_row": vmem((1, width), F32),
        "scaled": vmem((ndp, width), BF16),
        "normed": vmem((2, ndp, width), F32),
        "inv_std": vmem((2, ndp, 1), F32),
        "gs_own": vmem((2, ndp, width), BF16),
        "mx_own": vmem((2, ndp, width), BF16),
        "rows": vmem((2, ndp, width), BF16),
        "mine": vmem((8, tall, half), F32),
        "total": vmem((2, tall, block), F32),
        "bsum": vmem((4, tall, block), F32),
        "last_out": vmem((strip, half), F32),
        "last_in": vmem((strip, half), F32),
        "last_sem": DMA((2,)),
    }

    def both_ways(name, shape, count):
        scratch[name + "_out"] = vmem(shape, BF16)
        scratch[name + "_in"] = vmem(shape, BF16)
        scratch[name + "_ss"] = DMA((count,))
        scratch[name + "_rs"] = DMA((count,))

    for prefix in "ab":
        for i in "0123":
            both_ways(prefix + i + "z", (nz, GROUP, width // 2), 1)
            both_ways(prefix + i + "j", (GROUP, nz, width // 2), 1)
    for name, count in (("fr", 4), ("gs", 4), ("mx", 2)):
        both_ways(name, (2, ndp, width), count)
    both_ways("sib", (8, tall, half), 4)
    both_ways("a1", (2, tall, block), 2)
    both_ways("a2", (4, tall, block), 4)
    both_ways("b1", (2, tall // 2, block), 2)
    both_ways("b2", (4, tall // 2, block), 4)
    both_ways("ax", (tall, block), 1)
    both_ways("bx", (4, tall, block), 4)
    both_ways("s0", (nz, strip, block), 1)
    both_ways("s1", (nz, strip, block), 1)

    in_vmem = pl.BlockSpec(memory_space=pltpu.VMEM)
    anywhere = pl.BlockSpec(memory_space=pl.ANY)
    from_hbm = ("weight_in", "weight_out", "cotangent")
    results = pl.pallas_call(
        functools.partial(kernel, ndp, list(inputs) + list(outputs) + list(scratch)),
        out_shape=list(outputs.values()),
        in_specs=[anywhere if name in from_hbm else in_vmem for name in inputs],
        out_specs=[in_vmem] * 3,
        scratch_shapes=list(scratch.values()),
        compiler_params=pltpu.CompilerParams(
            collective_id=1, has_side_effects=True, vmem_limit_bytes=60 * 1024 * 1024
        ),
        name="module",
    )(*inputs.values())
    mixed, grad_source, grad_out = pl.pallas_call(
        finish_kernel,
        out_shape=list(outputs.values()),
        in_specs=[in_vmem] * 3,
        out_specs=[in_vmem] * 3,
        name="finish",
    )(*results)
    return (mixed, grad_source, grad_out.T)


def solution(mesh):
    return jax.shard_map(
        local,
        mesh=mesh,
        in_specs=(
            P(("dp", "tensor"), None),
            P(("dp", "tensor"), None),
            P(("dp", "tensor")),
            P(),
            P(None, "tensor"),
            P("tensor", None),
            P(("dp", "tensor"), None),
        ),
        out_specs=(P(("dp", "tensor"), None), P(("dp", "tensor"), None), P("tensor", "dp")),
        check_vma=False,
    )
```
